512 devices in a mesh: row: 16 (over y, x), col: 32 (over z, core).
Axes of the slice: x: 4, y: 4, z: 16, core: 2. Of those that a mesh axis runs over, the one named last changes fastest.
Arguments:
- pattern: int32 [64, 32], P('row', 'col'), may hold values from 0 to 1, as said below
- values: bfloat16 [64, 32, 128, 128], P('row', 'col'), as said below
- branch_sign: int32 [1], replicated, may hold values from 0 to 65535
Outputs:
- purified: float32 [64, 64, 128, 128], P('row', 'col')
- occupation: float32 [], replicated
The draws below stay inside these ranges and needn't reach their ends.
Inputs may be any that keep to these rules, and one draw needn't show every extreme that they name: Each block row stores exactly one block in each group of 2 block columns; the pattern is symmetric (block (i, j) is stored exactly when block (j, i) is), and every diagonal block is stored. `values`: X is symmetric: block (i, j) equals the transpose of block (j, i). `branch_sign`: an odd code selects the squaring branch, an even one the branch 2 X - X squared.
All inputs are finite; a program needn't handle non-finite values.
Results may differ from the reference program's by a relative error of at most 0.00115.
Values may be sent and summed in bfloat16 or wider, within the bound.
A program may use at most 64 MiB of HBM per device.

```python
import math
import jax
import jax.numpy as jnp
from jax import lax

BLK = 128
BC = 2
NB = 64
ORDER = 8192
N_COL = 32


def shared_pattern(key):
    perm_keys = jax.random.split(key, N_COL * N_COL)
    perm_table = jax.vmap(lambda one_key: jax.random.permutation(one_key, BC))(perm_keys)
    perm_table = perm_table.astype(jnp.int32).reshape(N_COL, N_COL, BC)
    row_ids = jnp.arange(NB, dtype=jnp.int32)
    row_group = row_ids // BC
    row_local = row_ids % BC
    col_groups = jnp.arange(N_COL, dtype=jnp.int32)
    lower_grp = jnp.minimum(row_group[:, None], col_groups[None, :])
    upper_grp = jnp.maximum(row_group[:, None], col_groups[None, :])
    chosen = perm_table[lower_grp, upper_grp]
    inverse = jnp.argsort(chosen, axis=-1).astype(jnp.int32)
    pick = jnp.broadcast_to(row_local[:, None, None], (NB, N_COL, 1))
    forward_ids = jnp.take_along_axis(chosen, pick, axis=2)[:, :, 0]
    backward_ids = jnp.take_along_axis(inverse, pick, axis=2)[:, :, 0]
    above = col_groups[None, :] > row_group[:, None]
    below = col_groups[None, :] < row_group[:, None]
    same_local = jnp.broadcast_to(row_local[:, None], (NB, N_COL))
    return jnp.where(above, forward_ids, jnp.where(below, backward_ids, same_local)).astype(jnp.int32)


def draw_pattern(key, part):
    pattern_table = shared_pattern(key)
    return pattern_table


def draw_values(key, part):
    pattern_table = shared_pattern(key)
    key = jax.random.fold_in(key, 2)
    noise_key, scale_key = jax.random.split(key)
    noise_blocks = jax.random.normal(noise_key, (NB, N_COL, BLK, BLK), jnp.float32) * 0.0085
    spread = jax.random.uniform(scale_key, (NB,), jnp.float32, 0.0, math.log(3.0)) - 0.5 * math.log(3.0)
    row_ids = jnp.arange(NB, dtype=jnp.int32)
    row_group = row_ids // BC
    col_groups = jnp.arange(N_COL, dtype=jnp.int32)
    global_cols = col_groups[None, :] * BC + pattern_table
    row_weight = (1.0 + 2.0 * row_ids.astype(jnp.float32) / (NB - 1)) * jnp.exp(spread)
    mirror = noise_blocks[global_cols, jnp.broadcast_to(row_group[:, None], (NB, N_COL))]
    symmetric = 0.5 * (noise_blocks + jnp.swapaxes(mirror, 2, 3))
    on_diag = (col_groups[None, :] == row_group[:, None]).astype(jnp.float32)
    symmetric = symmetric + 0.5 * on_diag[:, :, None, None] * jnp.eye(BLK, dtype=jnp.float32)[None, None]
    pair_scale = jnp.sqrt(row_weight[:, None] * row_weight[global_cols])
    return (symmetric * pair_scale[:, :, None, None]).astype(jnp.bfloat16)


def setup_inputs(seed: int = 0) -> dict:
    keys = jax.random.split(jax.random.key(seed), 4)
    pattern = draw_pattern(jax.random.fold_in(keys[3], 71), 0)
    values = draw_values(jax.random.fold_in(keys[3], 71), 0)
    branch_sign = jax.random.randint(keys[2], (1,), 0, 65536).astype(jnp.int32)
    return {"pattern": pattern, "values": values, "branch_sign": branch_sign}


def reference(pattern, values, branch_sign):
    places = jnp.arange(BC, dtype=jnp.int32)
    col_groups = jnp.arange(N_COL, dtype=jnp.int32)
    global_cols = col_groups[None, :] * BC + pattern
    odd_sign = branch_sign[0] % 2 == 1

    def one_row(row_id):
        own_blocks = values[row_id].astype(jnp.float32)
        inner_ids = global_cols[row_id]
        partner = values[inner_ids].astype(jnp.float32)
        partner_spot = pattern[inner_ids]
        products = jnp.einsum("cab,cqbd->cqad", own_blocks, partner, precision=lax.Precision.HIGHEST)
        placing = (partner_spot[:, :, None] == places[None, None, :]).astype(jnp.float32)
        square = jnp.einsum("cqad,cqp->qpad", products, placing, precision=lax.Precision.HIGHEST)
        own_place = (pattern[row_id][:, None] == places[None, :]).astype(jnp.float32)
        dense_row = own_place[:, :, None, None] * own_blocks[:, None, :, :]
        purified_row = jnp.where(odd_sign, square, 2.0 * dense_row - square)
        diag_block = purified_row[row_id // BC, row_id % BC]
        return purified_row.reshape(NB, BLK, BLK), jnp.trace(diag_block)

    purified, diag_traces = lax.map(one_row, jnp.arange(NB, dtype=jnp.int32))
    occupation = jnp.sum(diag_traces) / ORDER
    return purified, occupation
```

```python
import functools

import jax
import jax.numpy as jnp
from jax import lax
from jax.experimental import pallas as pl
from jax.experimental.pallas import tpu as pltpu
from jax.sharding import PartitionSpec as P

MESH = pl.DeviceIdType.MESH
NX, NY, NZ = 4, 4, 16
BLK = 128
ROWS = 4
META = ROWS * BLK
CHUNK = META + 16
SPLIT = 2 * BLK
PIECES = ((0, SPLIT), (SPLIT, CHUNK - SPLIT))
F32 = jnp.float32
BF16 = jnp.bfloat16


def kernel(pat_ref, sign_ref, val_ref, out_ref, occ_ref,
           zbuf, pbuf, lhs, rhs, tot, part, load_sem,
           z_send, z_recv, s_send, s_recv, p_send, p_recv, t_send, t_recv):
    row = lax.axis_index("row")
    col = lax.axis_index("col")
    y, x = row // NX, row % NX
    z, core = col // 2, col % 2
    sgn = 1 - 2 * core

    def at_z(dz):
        return (row, ((z + dz + NZ) % NZ) * 2 + core)

    def at_xy(dx, dy):
        return (((y + dy + NY) % NY) * NX + (x + dx + NX) % NX, col)

    sibling = (row, z * 2 + 1 - core)

    def slot_z(dz):
        return (z + dz + NZ) % NZ

    def slot_xy(dx, dy):
        return ((y + dy + NY) % NY) * NX + (x + dx + NX) % NX

    loads = []
    for n, (lo, ln) in enumerate(((0, SPLIT), (SPLIT, META - SPLIT))):
        src = val_ref.at[pl.ds(lo, ln)]
        loads.append(pltpu.make_async_copy(src, zbuf.at[z, core, pl.ds(lo, ln)], load_sem.at[n]))
        loads.append(pltpu.make_async_copy(src, pbuf.at[row, pl.ds(lo, ln)], load_sem.at[2 + n]))
    for load in loads:
        load.start()

    barrier = pltpu.get_barrier_semaphore()
    greet = [at_z(d) for d in (-1, 1, -2, -3, -4, -8, -12)]
    greet += [at_xy(1, 0), at_xy(-1, 0), at_xy(0, 1), at_xy(0, -1), sibling]
    for peer in greet:
        pl.semaphore_signal(barrier, inc=1, device_id=peer, device_id_type=MESH)

    for load in loads:
        load.wait()

    odd = (sign_ref[0] % 2).astype(F32)
    squares = jnp.zeros((8, BLK), F32)
    diag = jnp.zeros((8, BLK), F32)
    r_ids = lax.broadcasted_iota(jnp.int32, (BLK, BLK), 0)
    c_ids = lax.broadcasted_iota(jnp.int32, (BLK, BLK), 1)
    eye = (r_ids == c_ids).astype(F32)
    for i in range(ROWS):
        blk = zbuf[z, core, pl.ds(i * BLK, BLK), :].astype(F32)
        squares += jnp.sum((blk * blk).reshape(BLK // 8, 8, BLK), axis=0)
        on_diag = (col == row * 2 + i // 2).astype(F32)
        diag += jnp.sum((blk * eye).reshape(BLK // 8, 8, BLK), axis=0) * on_diag
    mine = (2.0 * odd - 1.0) * squares + (2.0 - 2.0 * odd) * diag
    mine = jnp.sum(mine, axis=0, keepdims=True)
    hi = mine.astype(BF16).astype(F32)
    mid = (mine - hi).astype(BF16).astype(F32)
    low = mine - hi - mid
    tile_row = lax.broadcasted_iota(jnp.int32, (16, BLK), 0)
    meta = jnp.zeros((16, BLK), F32)
    for i in range(ROWS):
        meta = jnp.where(tile_row == i, pat_ref[i, 0].astype(F32), meta)
    for i, term in enumerate((hi, mid, low)):
        meta = jnp.where(tile_row == ROWS + i, jnp.broadcast_to(term, (16, BLK)), meta)
    meta = meta.astype(BF16)
    zbuf[z, core, pl.ds(META, 16), :] = meta
    pbuf[row, pl.ds(META, 16), :] = meta

    pl.semaphore_wait(barrier, len(greet))

    sent = []

    def send(src, dst, send_sem, recv_sem, peer):
        copy = pltpu.make_async_remote_copy(
            src_ref=src, dst_ref=dst, send_sem=send_sem, recv_sem=recv_sem,
            device_id=peer, device_id_type=MESH)
        copy.start()
        sent.append(copy)

    def arrived(dst, sem):
        pltpu.make_async_copy(dst, dst, sem).wait()

    def z_ref(dz, who, n):
        lo, ln = PIECES[n]
        return zbuf.at[slot_z(dz), who, pl.ds(lo, ln)]

    def z_send_on(way, step, n):
        dz = -step if way == 0 else step
        src = z_ref(dz, core, n)
        send(src, src, z_send.at[way, step, n], z_recv.at[way, step + 1, n], at_z(1 - 2 * way))

    def s_index(way, step):
        return step if way == 0 else (NZ - step) % NZ

    def to_sibling(way, step, n):
        dz = -step if way == 0 else step
        src = z_ref(dz, core, n)
        k = s_index(way, step)
        send(src, src, s_send.at[k, n], s_recv.at[k, n], sibling)

    def from_sibling(way, step, n):
        dz = -step if way == 0 else step
        arrived(z_ref(dz, 1 - core, n), s_recv.at[s_index(way, step), n])

    def z_step(way, step, n):
        dz = -step if way == 0 else step
        arrived(z_ref(dz, core, n), z_recv.at[way, step, n])
        if step < NZ // 2 - 1 or (step == NZ // 2 - 1 and n == way):
            z_send_on(way, step, n)
        to_sibling(way, step, n)

    def forward(n):
        return sgn if n == 0 else -sgn

    def p_xy(n, a, b):
        f = forward(n)
        return (a * f, b * f) if n == 0 else (b * f, a * f)

    def p_ref(n, a, b):
        lo, ln = PIECES[n]
        return pbuf.at[slot_xy(*p_xy(n, a, b)), pl.ds(lo, ln)]

    AT = {0: 0, -1: 1, 1: 2, 2: 3}

    def p_sem(a, b):
        return AT[a] * 4 + AT[b]

    def p_send_a(n, a, way):
        there = a - way if a - way != -2 else 2
        send(p_ref(n, a, 0), p_ref(n, a, 0), p_send.at[n, p_sem(a, 0), (way + 1) // 2],
             p_recv.at[n, p_sem(there, 0)], at_xy(*p_xy(n, way, 0)))

    def p_send_b(n, a, b, way):
        there = b - way if b - way != -2 else 2
        send(p_ref(n, a, b), p_ref(n, a, b), p_send.at[n, p_sem(a, b), 2 + (way + 1) // 2],
             p_recv.at[n, p_sem(a, there)], at_xy(*p_xy(n, 0, way)))

    def p_arrived(n, a, b):
        arrived(p_ref(n, a, b), p_recv.at[n, p_sem(a, b)])

    def p_first(n, a):
        if a:
            p_arrived(n, a, 0)
        if a == -1:
            p_send_a(n, a, 1)
        p_send_b(n, a, 0, 1)
        p_send_b(n, a, 0, -1)

    def p_second(n, a):
        p_arrived(n, a, -1)
        p_send_b(n, a, -1, 1)

    for n in range(2):
        z_send_on(0, 0, n)
        z_send_on(1, 0, n)
        p_send_a(n, 0, 1)
        p_send_a(n, 0, -1)
    for n in range(2):
        p_first(n, 0)
        to_sibling(0, 0, n)

    def compute(shifts):
        for k, dz in enumerate(shifts):
            slot = slot_z(dz)
            for who in range(2):
                marks = zbuf[slot, who, pl.ds(META, 16), :].astype(F32)
                for i in range(ROWS):
                    spot = jnp.broadcast_to(marks[i:i + 1], (BLK, BLK)).astype(BF16)
                    blk = zbuf[slot, who, pl.ds(i * BLK, BLK), :]
                    at = (k * 2 + who) * 2 * BLK
                    lhs[i * BLK:(i + 1) * BLK, at:at + BLK] = blk * (1 - spot)
                    lhs[i * BLK:(i + 1) * BLK, at + BLK:at + 2 * BLK] = blk * spot
            marks = pbuf[slot, pl.ds(META, 16), :].astype(F32)
            for i in range(ROWS):
                spot = jnp.broadcast_to(marks[i:i + 1], (BLK, BLK)).astype(BF16)
                blk = pbuf[slot, pl.ds(i * BLK, BLK), :]
                at = (k * ROWS + i) * BLK
                rhs[at:at + BLK, :BLK] = blk * (1 - spot)
                rhs[at:at + BLK, BLK:] = blk * spot
        depth = len(shifts) * ROWS * BLK
        prod = jnp.dot(lhs[:, :depth], rhs[:depth, :], preferred_element_type=F32)
        for i in range(ROWS):
            for j in range(2):
                out_ref[i, j] += prod[i * BLK:(i + 1) * BLK, j * BLK:(j + 1) * BLK]

    def z_all(step, n):
        z_step(0, step, n)
        z_step(1, step, n)

    out_ref[...] = jnp.zeros_like(out_ref)

    z_all(1, 0)
    p_first(0, -1)
    p_first(1, -1)
    z_all(1, 1)
    p_first(0, 1)
    p_first(1, 1)

    z_all(2, 0)
    p_first(0, 2)
    p_first(1, 2)
    z_all(2, 1)
    p_second(0, 0)
    p_second(1, 0)

    z_all(3, 0)
    p_second(0, -1)
    p_second(1, -1)
    z_all(3, 1)
    p_second(0, 1)
    p_second(1, 1)

    z_all(4, 0)
    p_second(0, 2)
    p_second(1, 2)
    z_all(4, 1)

    z_all(5, 0)
    for n in range(2):
        for a in (0, -1, 1, 2):
            p_arrived(n, a, 1)
            p_arrived(n, a, 2)

    total = jnp.zeros((1, BLK), F32)
    for slot in range(NX * NY):
        marks = pbuf[slot, pl.ds(META, 16), :].astype(F32)
        total += (marks[ROWS:ROWS + 1] + marks[ROWS + 1:ROWS + 2]) + marks[ROWS + 2:ROWS + 3]

    def put(k, vec):
        tot[k] = jnp.broadcast_to(vec, (8, BLK))

    put(0, total)
    send(tot.at[0], part.at[0], t_send.at[0], t_recv.at[0], sibling)
    z_all(5, 1)

    def ready(step):
        for n in range(2):
            from_sibling(0, step, n)
            if 0 < step < NZ // 2:
                from_sibling(1, step, n)

    ready(0)
    ready(1)
    compute((0,))
    compute((-1, 1))
    arrived(part.at[0], t_recv.at[0])
    total += part[0][:1]
    put(1, total)
    for k in range(3):
        send(tot.at[1], part.at[1 + k], t_send.at[1 + k], t_recv.at[1 + k], at_z(1 + k))
    z_all(6, 0)
    ready(2)
    compute((-2, 2))
    z_all(6, 1)
    ready(3)
    compute((-3, 3))
    for k in range(3):
        arrived(part.at[1 + k], t_recv.at[1 + k])
        total += part[1 + k][:1]
    put(2, total)
    for k in range(3):
        send(tot.at[2], part.at[4 + k], t_send.at[4 + k], t_recv.at[4 + k], at_z((4, 8, 12)[k]))
    z_all(7, 0)
    ready(4)
    compute((-4, 4))
    z_all(7, 1)
    ready(5)
    compute((-5, 5))
    ready(6)
    compute((-6, 6))
    for k in range(3):
        arrived(part.at[4 + k], t_recv.at[4 + k])
        total += part[4 + k][:1]
    occ_ref[...] = jnp.broadcast_to(
        jnp.sum(total, axis=1, keepdims=True) / (NX * NY * ROWS * BLK), occ_ref.shape)
    z_step(0, 8, 0)
    z_step(1, 8, 1)
    ready(7)
    compute((-7, 7))
    ready(8)
    compute((8,))
    for copy in sent:
        copy.wait_send()


def on_device(pattern, values, branch_sign):
    square, occupation = pl.pallas_call(
        kernel,
        out_shape=(
            jax.ShapeDtypeStruct((ROWS, 2, BLK, BLK), F32),
            jax.ShapeDtypeStruct((8, BLK), F32),
        ),
        in_specs=[
            pl.BlockSpec(memory_space=pltpu.SMEM),
            pl.BlockSpec(memory_space=pltpu.SMEM),
            pl.BlockSpec(memory_space=pl.ANY),
        ],
        out_specs=(
            pl.BlockSpec(memory_space=pltpu.VMEM),
            pl.BlockSpec(memory_space=pltpu.VMEM),
        ),
        scratch_shapes=[
            pltpu.VMEM((NZ, 2, CHUNK, BLK), BF16),
            pltpu.VMEM((NX * NY, CHUNK, BLK), BF16),
            pltpu.VMEM((ROWS * BLK, 2 * ROWS * BLK), BF16),
            pltpu.VMEM((2 * ROWS * BLK, 2 * BLK), BF16),
            pltpu.VMEM((3, 8, BLK), F32),
            pltpu.VMEM((7, 8, BLK), F32),
            pltpu.SemaphoreType.DMA((4,)),
            pltpu.SemaphoreType.DMA((2, 8, 2)),
            pltpu.SemaphoreType.DMA((2, 9, 2)),
            pltpu.SemaphoreType.DMA((NZ, 2)),
            pltpu.SemaphoreType.DMA((NZ, 2)),
            pltpu.SemaphoreType.DMA((2, 16, 4)),
            pltpu.SemaphoreType.DMA((2, 16)),
            pltpu.SemaphoreType.DMA((7,)),
            pltpu.SemaphoreType.DMA((7,)),
        ],
        compiler_params=pltpu.CompilerParams(
            collective_id=0, has_side_effects=True, vmem_limit_bytes=32 * 1024 * 1024),
        cost_estimate=pl.CostEstimate(flops=2 * 512 * 8192 * 256, bytes_accessed=1 << 20, transcendentals=0),
    )(pattern, branch_sign, values.reshape(ROWS * BLK, BLK))
    spots = jnp.arange(2, dtype=jnp.int32)
    own = jnp.where((pattern == spots[None, :])[:, :, None, None], values.astype(F32), 0.0)
    odd = branch_sign[0] % 2 == 1
    purified = jnp.where(odd, square, 2.0 * own - square)
    return purified, occupation[0, 0]


def solution(mesh):
    in_specs = (P("row", "col"), P("row", "col", None, None), P())
    out_specs = (P("row", "col", None, None), P())
    return jax.shard_map(
        on_device, mesh=mesh, in_specs=in_specs, out_specs=out_specs, check_vma=False)
```

```python
import jax
import jax.numpy as jnp
from jax import lax
from jax.experimental import pallas as pl
from jax.experimental.pallas import tpu as pltpu
from jax.sharding import PartitionSpec as P

MESH = pl.DeviceIdType.MESH
NX, NY, NZ = 4, 4, 16
BLK = 128
ROWS = 4
PAIR = 2 * BLK
HALF = PAIR + 16
FAR = NZ // 2
F32 = jnp.float32
BF16 = jnp.bfloat16


def kernel(pat_ref, sign_ref, val_ref, out_ref, occ_ref,
           zbuf, pbuf, lhs, rhs, tot, part, load_sem, own_sem,
           z_send, z_recv, s_send, s_recv, p_send, p_recv, q_send, q_recv, t_send, t_recv):
    row = lax.axis_index("row")
    col = lax.axis_index("col")
    y, x = row // NX, row % NX
    z, core = col // 2, col % 2

    def slot_z(dz):
        return (z + dz + NZ) % NZ

    def slot_xy(dx, dy):
        return ((y + dy + NY) % NY) * NX + (x + dx + NX) % NX

    def at_z(dz, who):
        return (row, slot_z(dz) * 2 + who)

    def at_xy(dx, dy, who):
        return (slot_xy(dx, dy), z * 2 + who)

    sibling = (row, z * 2 + 1 - core)

    loads = [
        pltpu.make_async_copy(
            val_ref.at[pl.ds(n * PAIR, PAIR)], zbuf.at[z, core, n, pl.ds(0, PAIR)], load_sem.at[n])
        for n in range(2)
    ]
    for load in loads:
        load.start()

    barrier = pltpu.get_barrier_semaphore()

    def greet(peers):
        for peer in peers:
            pl.semaphore_signal(barrier, inc=1, device_id=peer, device_id_type=MESH)

    greet([sibling])

    @pl.when(core == 1)
    def _():
        greet([at_z(d, who) for d in (-1, 1) for who in range(2)])

    @pl.when(core == 0)
    def _():
        greet([at_xy(dx, dy, who) for dx, dy in ((1, 0), (-1, 0), (0, 1), (0, -1)) for who in range(2)])
        greet([at_xy(2, 0, 0), at_xy(0, 2, 0)])

    for load in loads:
        load.wait()

    odd = (sign_ref[0] % 2).astype(F32)
    sign = 2.0 * odd - 1.0
    squares = jnp.zeros((8, BLK), F32)
    diag = jnp.zeros((8, BLK), F32)
    eye = (lax.broadcasted_iota(jnp.int32, (BLK, BLK), 0)
           == lax.broadcasted_iota(jnp.int32, (BLK, BLK), 1)).astype(F32)
    tile_row = lax.broadcasted_iota(jnp.int32, (16, BLK), 0)
    for n in range(2):
        meta = jnp.zeros((16, BLK), F32)
        for k in range(2):
            i = 2 * n + k
            spot = pat_ref[0, i].astype(F32)
            meta = jnp.where(tile_row == k, spot, meta)
            blk = zbuf[z, core, n, k * BLK:(k + 1) * BLK, :].astype(F32)
            squares += jnp.sum((blk * blk).reshape(BLK // 8, 8, BLK), axis=0)
            on_diag = (col == row * 2 + n).astype(F32)
            diag += jnp.sum((blk * eye).reshape(BLK // 8, 8, BLK), axis=0) * on_diag
            twice = blk * (2.0 - 2.0 * odd)
            out_ref[i, 0] = twice * (1.0 - spot)
            out_ref[i, 1] = twice * spot
        zbuf[z, core, n, PAIR:, :] = meta.astype(BF16)
    tot[0] = sign * squares + (2.0 - 2.0 * odd) * diag

    @pl.when(core == 0)
    def _():
        pl.semaphore_wait(barrier, 7 + 2)

    @pl.when(core == 1)
    def _():
        pl.semaphore_wait(barrier, 7)

    def send(src, dst, send_sem, recv_sem, peer):
        pltpu.make_async_remote_copy(
            src_ref=src, dst_ref=dst, send_sem=send_sem, recv_sem=recv_sem,
            device_id=peer, device_id_type=MESH).start()

    def done(ref, sem):
        pltpu.make_async_copy(ref, ref, sem).wait()

    piece = zbuf.at[0, 0, 0]
    tile = tot.at[0]

    def z_ref(dz, who, n):
        return zbuf.at[slot_z(dz), who, n]

    def z_shift(way, step):
        return step * (2 * way - 1)

    def z_on(way, step, who, n):
        src = z_ref(z_shift(way, step), who, n)
        send(src, src, z_send.at[way, step, who, n], z_recv.at[way, step + 1, who, n], at_z(1 - 2 * way, 1))

    def z_share(dz, who, n):
        src = z_ref(dz, who, n)
        k = (dz + NZ) % NZ
        send(src, src, s_send.at[k, who, n], s_recv.at[k, who, n], sibling)

    def z_step(step, ways_on):
        for n in range(2):
            for who in range(2):
                for way in range(2):
                    done(piece, z_recv.at[way, step, who, n])
                    if ways_on(way, n):
                        z_on(way, step, who, n)
                    z_share(z_shift(way, step), who, n)

    def p_xy(who, n, a, b):
        f = (1 - 2 * who) * (1 - 2 * n)
        return f * ((1 - n) * a + n * b), f * ((1 - n) * b + n * a)

    def p_ref(who, n, a, b):
        return pbuf.at[who, slot_xy(*p_xy(who, n, a, b)), n]

    def p_at(a):
        return (a + 4) % 4

    def p_first(src, who, n, a, way):
        send(src, p_ref(who, n, a, 0), p_send.at[who, n, p_at(a), 0, (way + 1) // 2],
             p_recv.at[who, n, p_at(a - way), 0], at_xy(*p_xy(who, n, way, 0), 0))

    def p_second(src, who, n, a, b, way):
        send(src, p_ref(who, n, a, b), p_send.at[who, n, p_at(a), p_at(b), 2 + (way + 1) // 2],
             p_recv.at[who, n, p_at(a), p_at(b - way)], at_xy(*p_xy(who, n, 0, way), 0))

    def p_share(who, n, a, b):
        @pl.when(who == 1)
        def _():
            src = p_ref(who, n, a, b)
            send(src, src, q_send.at[n, p_at(a), p_at(b)], q_recv.at[n, p_at(a), p_at(b)], sibling)

    def each(body):
        def step(i, carry):
            body(i // 2, i % 2)
            return carry
        lax.fori_loop(0, 4, step, 0)

    for n in range(2):
        mine = zbuf.at[z, core, n]
        z_on(0, 0, core, n)
        z_on(1, 0, core, n)
        for way in (1, -1):
            p_first(mine, core, n, 0, way)
            p_second(mine, core, n, 0, 0, way)
    for n in range(2):
        z_share(0, core, n)
    own_copies = [
        pltpu.make_async_copy(zbuf.at[z, core, n], pbuf.at[core, row, n], own_sem.at[n]) for n in range(2)]
    for copy in own_copies:
        copy.start()

    def t_copy(k, src, peer):
        send(tot.at[src], part.at[k], t_send.at[k], t_recv.at[k], peer)

    def t_add(src, dst, ks):
        total = tot[src]
        for k in ks:
            done(tile, t_recv.at[k])
            total += part[k]
        tot[dst] = total

    def spread(i):
        return ((i + 1) // 2) * (1 - 2 * (i % 2))

    def compute(i):
        slot = slot_z(spread(i))
        for n in range(2):
            for who in range(2):
                marks = zbuf[slot, who, n, PAIR:, :].astype(F32)
                for k in range(2):
                    spot = jnp.broadcast_to(marks[k:k + 1], (16, BLK)) * sign
                    blk = zbuf[slot, who, n, k * BLK:(k + 1) * BLK, :].reshape(BLK // 16, 16, BLK)
                    r, c = (2 * n + k) * BLK, who * PAIR
                    lhs[r:r + BLK, c:c + BLK] = (blk * (sign - spot).astype(BF16)[None]).reshape(BLK, BLK)
                    lhs[r:r + BLK, c + BLK:c + PAIR] = (blk * spot.astype(BF16)[None]).reshape(BLK, BLK)
            marks = pbuf[core, slot, n, PAIR:, :].astype(F32)
            for k in range(2):
                spot = jnp.broadcast_to(marks[k:k + 1], (16, BLK))
                blk = pbuf[core, slot, n, k * BLK:(k + 1) * BLK, :].reshape(BLK // 16, 16, BLK)
                r = (2 * n + k) * BLK
                rhs[r:r + BLK, :BLK] = (blk * (1.0 - spot).astype(BF16)[None]).reshape(BLK, BLK)
                rhs[r:r + BLK, BLK:] = (blk * spot.astype(BF16)[None]).reshape(BLK, BLK)
        prod = jnp.dot(lhs[...], rhs[...], preferred_element_type=F32)
        for i in range(ROWS):
            for j in range(2):
                out_ref[i, j] += prod[i * BLK:(i + 1) * BLK, j * BLK:(j + 1) * BLK]

    def loop(lo, hi, body):
        def step(i, carry):
            body(i)
            return carry
        lax.fori_loop(lo, hi, step, 0)

    @pl.when(core == 1)
    def _():
        t_copy(0, 0, sibling)
        loop(1, 5, lambda step: z_step(step, lambda way, n: True))
        done(tile, t_recv.at[7])
        tot[1] = part[7]
        for k in range(3):
            t_copy(8 + k, 1, at_z(1 + k, 1))
        z_step(5, lambda way, n: True)
        t_add(1, 2, (8, 9, 10))
        t_copy(11, 2, at_z(4, 1))
        t_copy(12, 2, at_z(-4, 1))
        z_step(6, lambda way, n: True)
        done(tile, t_recv.at[11])
        send(part.at[11], part.at[13], t_send.at[13], t_recv.at[13], at_z(4, 1))

        def p_taken(who, n):
            @pl.when(who == 1)
            def _():
                for a in range(4):
                    for b in range(4):
                        if a or b:
                            done(piece, q_recv.at[n, a, b])
        z_step(7, lambda way, n: way == n)
        each(p_taken)
        for copy in own_copies:
            copy.wait()
        for n in range(2):
            done(piece, s_recv.at[0, 0, n])
        loop(0, 13, compute)
        t_tail = tot[2] + part[11]
        for k in (12, 13):
            done(tile, t_recv.at[k])
            t_tail += part[k]
        tot[3] = t_tail
        tot[4] = t_tail
        t_copy(14, 3, sibling)
        for n in range(2):
            for who in range(2):
                done(piece, z_recv.at[n, FAR, who, n])
                z_share(FAR, who, n)
        loop(13, 16, compute)

    @pl.when(core == 0)
    def _():
        def take(who, n, a, b):
            done(piece, p_recv.at[who, n, p_at(a), p_at(b)])
            p_share(who, n, a, b)

        def first(a):
            def body(who, n):
                done(piece, p_recv.at[who, n, p_at(a), 0])
                src = p_ref(who, n, a, 0)
                if a == -1:
                    p_first(src, who, n, a, 1)
                p_second(src, who, n, a, 0, 1)
                p_second(src, who, n, a, 0, -1)
                p_share(who, n, a, 0)
            each(body)

        def second(a):
            def body(who, n):
                done(piece, p_recv.at[who, n, p_at(a), p_at(-1)])
                p_second(p_ref(who, n, a, -1), who, n, a, -1, 1)
                p_share(who, n, a, -1)
            each(body)

        t_add(0, 1, (0,))
        for k in range(3):
            t_copy(1 + k, 1, at_xy(1 + k, 0, 0))
        first(-1)
        first(1)
        t_add(1, 2, (1, 2, 3))
        for k in range(3):
            t_copy(4 + k, 2, at_xy(0, 1 + k, 0))
        first(2)
        second(0)
        t_add(2, 3, (4, 5, 6))
        t_copy(7, 3, sibling)
        second(-1)
        second(1)
        second(2)
        for b in (1, 2):
            for a in (0, -1, 1, 2):
                each(lambda who, n, a=a, b=b: take(who, n, a, b))
        for copy in own_copies:
            copy.wait()

        def z_taken(i):
            k = (spread(i) + NZ) % NZ
            for n in range(2):
                for who in range(2):
                    done(piece, s_recv.at[k, who, n])
            compute(i)

        for n in range(2):
            done(piece, s_recv.at[0, 1, n])
        compute(0)
        loop(1, 16, z_taken)
        done(tile, t_recv.at[14])
        tot[4] = part[14]

    total = jnp.sum(jnp.sum(tot[4], axis=0, keepdims=True), axis=1, keepdims=True)
    occ_ref[...] = jnp.broadcast_to(total / (NX * NY * ROWS * BLK), occ_ref.shape)

    for n in range(2):
        for way in range(2):
            done(piece, z_send.at[way, 0, core, n])
            done(piece, p_send.at[core, n, 0, 0, way])
            done(piece, p_send.at[core, n, 0, 0, 2 + way])
        done(piece, s_send.at[0, core, n])

    @pl.when(core == 1)
    def _():
        def sent(step):
            for n in range(2):
                for who in range(2):
                    for way in range(2):
                        done(piece, z_send.at[way, step, who, n])
        loop(1, FAR - 1, sent)
        for n in range(2):
            for who in range(2):
                done(piece, z_send.at[n, FAR - 1, who, n])

        def shared(k):
            for n in range(2):
                for who in range(2):
                    done(piece, s_send.at[k, who, n])
        loop(1, NZ, shared)
        for k in (0, 8, 9, 10, 11, 12, 13, 14):
            done(tile, t_send.at[k])

    @pl.when(core == 0)
    def _():
        def sent(who, n):
            done(piece, p_send.at[who, n, 3, 0, 1])
            for a in range(4):
                if a:
                    done(piece, p_send.at[who, n, a, 0, 2])
                    done(piece, p_send.at[who, n, a, 0, 3])
                done(piece, p_send.at[who, n, a, 3, 3])

            @pl.when(who == 1)
            def _():
                for a in range(4):
                    for b in range(4):
                        if a or b:
                            done(piece, q_send.at[n, a, b])
        each(sent)
        for k in (1, 2, 3, 4, 5, 6, 7):
            done(tile, t_send.at[k])


def on_device(pattern, values, branch_sign):
    purified, occupation = pl.pallas_call(
        kernel,
        out_shape=(
            jax.ShapeDtypeStruct((ROWS, 2, BLK, BLK), F32),
            jax.ShapeDtypeStruct((8, BLK), F32),
        ),
        in_specs=[
            pl.BlockSpec(memory_space=pltpu.SMEM),
            pl.BlockSpec(memory_space=pltpu.SMEM),
            pl.BlockSpec(memory_space=pl.ANY),
        ],
        out_specs=(
            pl.BlockSpec(memory_space=pltpu.VMEM),
            pl.BlockSpec(memory_space=pltpu.VMEM),
        ),
        scratch_shapes=[
            pltpu.VMEM((NZ, 2, 2, HALF, BLK), BF16),
            pltpu.VMEM((2, NX * NY, 2, HALF, BLK), BF16),
            pltpu.VMEM((ROWS * BLK, ROWS * BLK), BF16),
            pltpu.VMEM((ROWS * BLK, PAIR), BF16),
            pltpu.VMEM((5, 8, BLK), F32),
            pltpu.VMEM((15, 8, BLK), F32),
            pltpu.SemaphoreType.DMA((2,)),
            pltpu.SemaphoreType.DMA((2,)),
            pltpu.SemaphoreType.DMA((2, FAR, 2, 2)),
            pltpu.SemaphoreType.DMA((2, FAR + 1, 2, 2)),
            pltpu.SemaphoreType.DMA((NZ, 2, 2)),
            pltpu.SemaphoreType.DMA((NZ, 2, 2)),
            pltpu.SemaphoreType.DMA((2, 2, 4, 4, 4)),
            pltpu.SemaphoreType.DMA((2, 2, 4, 4)),
            pltpu.SemaphoreType.DMA((2, 4, 4)),
            pltpu.SemaphoreType.DMA((2, 4, 4)),
            pltpu.SemaphoreType.DMA((15,)),
            pltpu.SemaphoreType.DMA((15,)),
        ],
        compiler_params=pltpu.CompilerParams(
            collective_id=0, has_side_effects=True, vmem_limit_bytes=32 * 1024 * 1024),
        cost_estimate=pl.CostEstimate(flops=2 * 512 * 8192 * 256, bytes_accessed=1 << 20, transcendentals=0),
    )(pattern.reshape(1, ROWS), branch_sign, values.reshape(ROWS * BLK, BLK))
    return purified, occupation[0, 0]


def solution(mesh):
    in_specs = (P("row", "col"), P("row", "col", None, None), P())
    out_specs = (P("row", "col", None, None), P())
    return jax.shard_map(
        on_device, mesh=mesh, in_specs=in_specs, out_specs=out_specs, check_vma=False)
```

```python
import jax
import jax.numpy as jnp
from jax import lax
from jax.experimental import pallas as pl
from jax.experimental.pallas import tpu as pltpu
from jax.sharding import PartitionSpec as P

MESH = pl.DeviceIdType.MESH
NX, NY, NZ = 4, 4, 16
BLK = 128
ROWS = 4
PAIR = 2 * BLK
HALF = PAIR + 16
FAR = NZ // 2
F32 = jnp.float32
BF16 = jnp.bfloat16


def kernel(pat_hbm, sign_ref, val_ref, out_ref, occ_ref,
           zbuf, pbuf, lhs, rhs, tot, part, pat_ref, load_sem, small_sem, own_sem,
           z_send, z_recv, s_send, s_recv, p_send, p_recv, q_send, q_recv, t_send, t_recv):
    row = lax.axis_index("row")
    col = lax.axis_index("col")
    y, x = row // NX, row % NX
    z, core = col // 2, col % 2

    def slot_z(dz):
        return (z + dz + NZ) % NZ

    def slot_xy(dx, dy):
        return ((y + dy + NY) % NY) * NX + (x + dx + NX) % NX

    def at_z(dz, who):
        return (row, slot_z(dz) * 2 + who)

    def at_xy(dx, dy, who):
        return (slot_xy(dx, dy), z * 2 + who)

    sibling = (row, z * 2 + 1 - core)

    barrier = pltpu.get_barrier_semaphore()

    def greet(peers):
        for peer in peers:
            pl.semaphore_signal(barrier, inc=1, device_id=peer, device_id_type=MESH)

    @pl.when(core == 1)
    def _():
        greet([at_z(-1, 1), at_z(1, 1)])

    greet([sibling])

    @pl.when(core == 0)
    def _():
        greet([at_xy(1, 0, 0), at_xy(-1, 0, 0), at_xy(0, 1, 0), at_xy(0, -1, 0), at_xy(2, 0, 0), at_xy(0, 2, 0)])

    small = pltpu.make_async_copy(pat_hbm, pat_ref, small_sem.at[0])
    small.start()
    loads = [
        pltpu.make_async_copy(
            val_ref.at[pl.ds(n * PAIR, PAIR)], zbuf.at[z, core, n, pl.ds(0, PAIR)], load_sem.at[n])
        for n in range(2)
    ]
    for load in loads:
        load.start()

    small.wait()
    odd = (sign_ref[0] % 2).astype(F32)
    sign = 2.0 * odd - 1.0
    spots = [pat_ref[0, i].astype(F32) for i in range(ROWS)]
    tile_row = lax.broadcasted_iota(jnp.int32, (16, BLK), 0)
    for n in range(2):
        marks = jnp.where(tile_row == 0, spots[2 * n], jnp.where(tile_row == 1, spots[2 * n + 1], 0.0))
        zbuf[z, core, n, PAIR:, :] = marks.astype(BF16)
    for load in loads:
        load.wait()

    @pl.when(core == 0)
    def _():
        pl.semaphore_wait(barrier, 7)

    @pl.when(core == 1)
    def _():
        pl.semaphore_wait(barrier, 3)

    def send(src, dst, send_sem, recv_sem, peer):
        pltpu.make_async_remote_copy(
            src_ref=src, dst_ref=dst, send_sem=send_sem, recv_sem=recv_sem,
            device_id=peer, device_id_type=MESH).start()

    def done(ref, sem):
        pltpu.make_async_copy(ref, ref, sem).wait()

    piece = zbuf.at[0, 0, 0]
    tile = tot.at[0]

    def z_ref(dz, who, n):
        return zbuf.at[slot_z(dz), who, n]

    def z_shift(way, step):
        return step * (2 * way - 1)

    def z_on(way, step, who, n):
        dst = z_ref(z_shift(way, step), who, n)
        send(dst, dst, z_send.at[way, step, who, n], z_recv.at[way, step + 1, who, n], at_z(1 - 2 * way, 1))

    def z_share(dz, who, n):
        dst = z_ref(dz, who, n)
        k = (dz + NZ) % NZ
        send(dst, dst, s_send.at[k, who, n], s_recv.at[k, who, n], sibling)

    def z_step(who, step, on=lambda way, n: True):
        for n in range(2):
            for way in range(2):
                done(piece, z_recv.at[way, step, who, n])
                if on(way, n):
                    z_on(way, step, who, n)
                z_share(z_shift(way, step), who, n)

    def z_last(who):
        for n in range(2):
            done(piece, z_recv.at[n, FAR, who, n])
            z_share(FAR, who, n)

    def last_hop(way, n):
        return way == n

    def z_sent(who, step):
        for n in range(2):
            for way in range(2):
                done(piece, z_send.at[way, step, who, n])

    def s_sent(who, step):
        for n in range(2):
            done(piece, s_send.at[NZ - step, who, n])
            done(piece, s_send.at[step, who, n])

    def p_xy(who, n, a, b):
        f = (1 - 2 * who) * (1 - 2 * n)
        return f * ((1 - n) * a + n * b), f * ((1 - n) * b + n * a)

    def p_ref(who, n, a, b):
        return pbuf.at[who, slot_xy(*p_xy(who, n, a, b)), n]

    def p_at(a):
        return (a + 4) % 4

    def p_first(src, who, n, a, way):
        send(src, p_ref(who, n, a, 0), p_send.at[who, n, p_at(a), 0, (way + 1) // 2],
             p_recv.at[who, n, p_at(a - way), 0], at_xy(*p_xy(who, n, way, 0), 0))

    def p_second(src, who, n, a, b, way):
        send(src, p_ref(who, n, a, b), p_send.at[who, n, p_at(a), p_at(b), 2 + (way + 1) // 2],
             p_recv.at[who, n, p_at(a), p_at(b - way)], at_xy(*p_xy(who, n, 0, way), 0))

    def p_share(who, n, a, b):
        @pl.when(who == 1)
        def _():
            src = p_ref(who, n, a, b)
            send(src, src, q_send.at[n, p_at(a), p_at(b)], q_recv.at[n, p_at(a), p_at(b)], sibling)

    def each(body):
        def step(i, carry):
            body(i // 2, i % 2)
            return carry
        lax.fori_loop(0, 4, step, 0)

    @pl.when(core == 1)
    def _():
        for n in range(2):
            z_on(0, 0, 1, n)
            z_on(1, 0, 1, n)

    for n in range(2):
        z_share(0, core, n)
    own_copies = [
        pltpu.make_async_copy(zbuf.at[z, core, n], pbuf.at[core, row, n], own_sem.at[n]) for n in range(2)]
    for copy in own_copies:
        copy.start()

    def own_part():
        squares = jnp.zeros((8, BLK), F32)
        diag = jnp.zeros((8, BLK), F32)
        eye = (lax.broadcasted_iota(jnp.int32, (BLK, BLK), 0)
               == lax.broadcasted_iota(jnp.int32, (BLK, BLK), 1)).astype(F32)
        for i in range(ROWS):
            n, k = i // 2, i % 2
            blk = zbuf[z, core, n, k * BLK:(k + 1) * BLK, :].astype(F32)
            squares += jnp.sum((blk * blk).reshape(BLK // 8, 8, BLK), axis=0)
            on_diag = (col == row * 2 + n).astype(F32)
            diag += jnp.sum((blk * eye).reshape(BLK // 8, 8, BLK), axis=0) * on_diag
            twice = blk * (2.0 - 2.0 * odd)
            out_ref[i, 0] = twice * (1.0 - spots[i])
            out_ref[i, 1] = twice * spots[i]
        tot[0] = sign * squares + (2.0 - 2.0 * odd) * diag

    def t_copy(k, src, peer):
        send(tot.at[src], part.at[k], t_send.at[k], t_recv.at[k], peer)

    def t_add(src, dst, ks):
        total = tot[src]
        for k in ks:
            done(tile, t_recv.at[k])
            total += part[k]
        tot[dst] = total

    def spread(i):
        return ((i + 1) // 2) * (1 - 2 * (i % 2))

    def compute(i, count):
        for g in range(count):
            slot = slot_z(spread(i + g))
            for n in range(2):
                for who in range(2):
                    marks = zbuf[slot, who, n, PAIR:, :].astype(F32)
                    for k in range(2):
                        spot = jnp.broadcast_to(marks[k:k + 1], (16, BLK)) * sign
                        blk = zbuf[slot, who, n, k * BLK:(k + 1) * BLK, :].reshape(BLK // 16, 16, BLK)
                        r, c = (2 * n + k) * BLK, (2 * g + who) * PAIR
                        lhs[r:r + BLK, c:c + BLK] = (blk * (sign - spot).astype(BF16)[None]).reshape(BLK, BLK)
                        lhs[r:r + BLK, c + BLK:c + PAIR] = (blk * spot.astype(BF16)[None]).reshape(BLK, BLK)
                marks = pbuf[core, slot, n, PAIR:, :].astype(F32)
                for k in range(2):
                    spot = jnp.broadcast_to(marks[k:k + 1], (16, BLK))
                    blk = pbuf[core, slot, n, k * BLK:(k + 1) * BLK, :].reshape(BLK // 16, 16, BLK)
                    r = (ROWS * g + 2 * n + k) * BLK
                    rhs[r:r + BLK, :BLK] = (blk * (1.0 - spot).astype(BF16)[None]).reshape(BLK, BLK)
                    rhs[r:r + BLK, BLK:] = (blk * spot.astype(BF16)[None]).reshape(BLK, BLK)
        depth = count * ROWS * BLK
        prod = jnp.dot(lhs[:, :depth], rhs[:depth, :], preferred_element_type=F32)
        for r in range(ROWS):
            for j in range(2):
                out_ref[r, j] += prod[r * BLK:(r + 1) * BLK, j * BLK:(j + 1) * BLK]

    def loop(lo, hi, body):
        def step(i, carry):
            body(i)
            return carry
        lax.fori_loop(lo, hi, step, 0)

    @pl.when(core == 1)
    def _():
        own_part()
        t_copy(0, 0, sibling)
        z_step(1, 1)
        for n in range(2):
            done(piece, s_recv.at[0, 0, n])
            z_on(0, 0, 0, n)
            z_on(1, 0, 0, n)
        z_sent(1, 0)

        def ring(step):
            z_step(1, step)
            z_step(0, step - 1)

            @pl.when(step == 5)
            def _():
                done(tile, t_recv.at[7])
                tot[1] = part[7]
                for k in range(3):
                    t_copy(8 + k, 1, at_z(1 + k, 1))

            @pl.when(step == 6)
            def _():
                t_add(1, 2, (8, 9, 10))
                t_copy(11, 2, at_z(4, 1))
                t_copy(12, 2, at_z(-4, 1))

            z_sent(1, step - 1)
            s_sent(1, step - 1)
            z_sent(0, step - 2)

            @pl.when(step > 2)
            def _():
                s_sent(0, step - 2)

        loop(2, 7, ring)
        for n in range(2):
            done(piece, s_send.at[0, 1, n])
            for a in range(4):
                for b in range(4):
                    if a or b:
                        done(piece, q_recv.at[n, a, b])
        for copy in own_copies:
            copy.wait()

    @pl.when(core == 0)
    def _():
        def p_begin(who, n):
            src = zbuf.at[z, who, n]
            for way in (1, -1):
                p_first(src, who, n, 0, way)
                p_second(src, who, n, 0, 0, way)

        def take(who, n, a, b):
            done(piece, p_recv.at[who, n, p_at(a), p_at(b)])
            p_share(who, n, a, b)

        def first(a):
            def body(who, n):
                done(piece, p_recv.at[who, n, p_at(a), 0])
                src = p_ref(who, n, a, 0)
                if a == -1:
                    p_first(src, who, n, a, 1)
                p_second(src, who, n, a, 0, 1)
                p_second(src, who, n, a, 0, -1)
                p_share(who, n, a, 0)
            each(body)

        def second(a):
            def body(who, n):
                done(piece, p_recv.at[who, n, p_at(a), p_at(-1)])
                p_second(p_ref(who, n, a, -1), who, n, a, -1, 1)
                p_share(who, n, a, -1)
            each(body)

        for n in range(2):
            p_begin(0, n)
        own_part()
        for n in range(2):
            done(piece, s_recv.at[0, 1, n])
            p_begin(1, n)
        t_add(0, 1, (0,))
        for k in range(3):
            t_copy(1 + k, 1, at_xy(1 + k, 0, 0))
        t_add(1, 2, (1, 2, 3))
        for k in range(3):
            t_copy(4 + k, 2, at_xy(0, 1 + k, 0))
        first(-1)
        first(1)
        t_add(2, 3, (4, 5, 6))
        t_copy(7, 3, sibling)
        first(2)
        second(0)
        second(-1)
        second(1)
        second(2)
        for b in (1, 2):
            for a in (0, -1, 1, 2):
                each(lambda who, n, a=a, b=b: take(who, n, a, b))
        for copy in own_copies:
            copy.wait()
        for n in range(2):
            done(piece, s_send.at[0, 0, n])

        def sent(who, n):
            done(piece, p_send.at[who, n, 3, 0, 1])
            done(piece, p_send.at[who, n, 0, 0, 0])
            done(piece, p_send.at[who, n, 0, 0, 1])
            for a in range(4):
                done(piece, p_send.at[who, n, a, 0, 2])
                done(piece, p_send.at[who, n, a, 0, 3])
                done(piece, p_send.at[who, n, a, 3, 3])

            @pl.when(who == 1)
            def _():
                for a in range(4):
                    for b in range(4):
                        if a or b:
                            done(piece, q_send.at[n, a, b])
        each(sent)
        for k in (1, 2, 3, 4, 5, 6, 7):
            done(tile, t_send.at[k])

    def z_taken(i, count):
        @pl.when(core == 0)
        def _():
            for g in range(count):
                for n in range(2):
                    for who in range(2):
                        done(piece, s_recv.at[(spread(i + g) + NZ) % NZ, who, n])

    def four(i):
        @pl.when((core == 1) & (i == 2))
        def _():
            z_step(1, 7, last_hop)
            z_step(0, 6)
            done(tile, t_recv.at[11])
            send(part.at[11], part.at[13], t_send.at[13], t_recv.at[13], at_z(4, 1))

        @pl.when((core == 0) & (i == 0))
        def _():
            for g in range(1, 4):
                for n in range(2):
                    for who in range(2):
                        done(piece, s_recv.at[(spread(g) + NZ) % NZ, who, n])

        @pl.when(i > 0)
        def _():
            z_taken(4 * i, 4)

        compute(4 * i, 4)

    loop(0, 3, four)

    @pl.when(core == 1)
    def _():
        z_last(1)
        z_step(0, 7, last_hop)

    z_taken(12, 2)
    compute(12, 2)

    def one(i):
        @pl.when((core == 1) & (i == 14))
        def _():
            z_last(0)
            z_sent(1, 6)
            z_sent(0, 5)
            z_sent(0, 6)
            s_sent(1, 6)
            s_sent(0, 5)

        z_taken(i, 1)
        compute(i, 1)

    loop(14, 16, one)

    @pl.when(core == 1)
    def _():
        tail = tot[2] + part[11]
        for k in (12, 13):
            done(tile, t_recv.at[k])
            tail += part[k]
        tot[3] = tail
        t_copy(14, 3, sibling)
        tot[4] = tail
        for who in range(2):
            for n in range(2):
                done(piece, z_send.at[n, FAR - 1, who, n])
                done(piece, s_send.at[FAR, who, n])
            s_sent(who, 7)
        s_sent(0, 6)
        for k in (0, 8, 9, 10, 11, 12, 13, 14):
            done(tile, t_send.at[k])

    @pl.when(core == 0)
    def _():
        done(tile, t_recv.at[14])
        tot[4] = part[14]

    total = jnp.sum(jnp.sum(tot[4], axis=0, keepdims=True), axis=1, keepdims=True)
    occ_ref[...] = jnp.broadcast_to(total / (NX * NY * ROWS * BLK), occ_ref.shape)


def on_device(pattern, values, branch_sign):
    purified, occupation = pl.pallas_call(
        kernel,
        out_shape=(
            jax.ShapeDtypeStruct((ROWS, 2, BLK, BLK), F32),
            jax.ShapeDtypeStruct((8, BLK), F32),
        ),
        in_specs=[
            pl.BlockSpec(memory_space=pltpu.HBM),
            pl.BlockSpec(memory_space=pltpu.SMEM),
            pl.BlockSpec(memory_space=pltpu.HBM),
        ],
        out_specs=(
            pl.BlockSpec(memory_space=pltpu.VMEM),
            pl.BlockSpec(memory_space=pltpu.VMEM),
        ),
        scratch_shapes=[
            pltpu.VMEM((NZ, 2, 2, HALF, BLK), BF16),
            pltpu.VMEM((2, NX * NY, 2, HALF, BLK), BF16),
            pltpu.VMEM((ROWS * BLK, 4 * ROWS * BLK), BF16),
            pltpu.VMEM((4 * ROWS * BLK, PAIR), BF16),
            pltpu.VMEM((5, 8, BLK), F32),
            pltpu.VMEM((15, 8, BLK), F32),
            pltpu.SMEM((1, ROWS), jnp.int32),
            pltpu.SemaphoreType.DMA((2,)),
            pltpu.SemaphoreType.DMA((1,)),
            pltpu.SemaphoreType.DMA((2,)),
            pltpu.SemaphoreType.DMA((2, FAR, 2, 2)),
            pltpu.SemaphoreType.DMA((2, FAR + 1, 2, 2)),
            pltpu.SemaphoreType.DMA((NZ, 2, 2)),
            pltpu.SemaphoreType.DMA((NZ, 2, 2)),
            pltpu.SemaphoreType.DMA((2, 2, 4, 4, 4)),
            pltpu.SemaphoreType.DMA((2, 2, 4, 4)),
            pltpu.SemaphoreType.DMA((2, 4, 4)),
            pltpu.SemaphoreType.DMA((2, 4, 4)),
            pltpu.SemaphoreType.DMA((15,)),
            pltpu.SemaphoreType.DMA((15,)),
        ],
        compiler_params=pltpu.CompilerParams(
            collective_id=0, has_side_effects=True, vmem_limit_bytes=32 * 1024 * 1024),
        cost_estimate=pl.CostEstimate(flops=2 * 512 * 8192 * 256, bytes_accessed=1 << 20, transcendentals=0),
    )(pltpu.with_memory_space_constraint(pattern.reshape(1, ROWS), pltpu.HBM), branch_sign,
      pltpu.with_memory_space_constraint(values.reshape(ROWS * BLK, BLK), pltpu.HBM))
    return purified, occupation[0, 0]


def solution(mesh):
    in_specs = (P("row", "col"), P("row", "col", None, None), P())
    out_specs = (P("row", "col", None, None), P())
    return jax.shard_map(
        on_device, mesh=mesh, in_specs=in_specs, out_specs=out_specs, check_vma=False)
```

```python
import jax
import jax.numpy as jnp
from jax import lax
from jax.experimental import pallas as pl
from jax.experimental.pallas import tpu as pltpu
from jax.sharding import PartitionSpec as P

MESH = pl.DeviceIdType.MESH
NX, NY, NZ = 4, 4, 16
BLK = 128
ROWS = 4
PAIR = 2 * BLK
HALF = PAIR + 16
FAR = NZ // 2
F32 = jnp.float32
BF16 = jnp.bfloat16


def kernel(pat_hbm, sign_ref, val_ref, out_ref, occ_ref,
           zbuf, pbuf, lhs, rhs, tot, part, pat_ref, load_sem, small_sem, own_sem,
           step_send, last_send, share_send, z_recv, s_recv, p_send, p_recv, q_send, q_recv, t_send, t_recv):
    row = lax.axis_index("row")
    col = lax.axis_index("col")
    y, x = row // NX, row % NX
    z, core = col // 2, col % 2

    def slot_z(dz):
        return (z + dz + NZ) % NZ

    def slot_xy(dx, dy):
        return ((y + dy + NY) % NY) * NX + (x + dx + NX) % NX

    def at_z(dz, who):
        return (row, slot_z(dz) * 2 + who)

    def at_xy(dx, dy, who):
        return (slot_xy(dx, dy), z * 2 + who)

    sibling = (row, z * 2 + 1 - core)

    barrier = pltpu.get_barrier_semaphore()

    def greet(peers):
        for peer in peers:
            pl.semaphore_signal(barrier, inc=1, device_id=peer, device_id_type=MESH)

    @pl.when(core == 1)
    def _():
        greet([at_z(-1, 1), at_z(1, 1)])

    greet([sibling])

    @pl.when(core == 0)
    def _():
        greet([at_xy(1, 0, 0), at_xy(-1, 0, 0), at_xy(0, 1, 0), at_xy(0, -1, 0), at_xy(2, 0, 0), at_xy(0, 2, 0)])

    small = pltpu.make_async_copy(pat_hbm, pat_ref, small_sem.at[0])
    small.start()
    loads = [
        pltpu.make_async_copy(
            val_ref.at[pl.ds(n * PAIR, PAIR)], zbuf.at[z, core, n, pl.ds(0, PAIR)], load_sem.at[n])
        for n in range(2)
    ]
    for load in loads:
        load.start()

    small.wait()
    odd = (sign_ref[0] % 2).astype(F32)
    sign = 2.0 * odd - 1.0
    spots = [pat_ref[0, i].astype(F32) for i in range(ROWS)]
    tile_row = lax.broadcasted_iota(jnp.int32, (16, BLK), 0)
    for n in range(2):
        marks = jnp.where(tile_row == 0, spots[2 * n], jnp.where(tile_row == 1, spots[2 * n + 1], 0.0))
        zbuf[z, core, n, PAIR:, :] = marks.astype(BF16)
    for load in loads:
        load.wait()

    @pl.when(core == 0)
    def _():
        pl.semaphore_wait(barrier, 7)

    @pl.when(core == 1)
    def _():
        pl.semaphore_wait(barrier, 3)

    def send(src, dst, send_sem, recv_sem, peer):
        pltpu.make_async_remote_copy(
            src_ref=src, dst_ref=dst, send_sem=send_sem, recv_sem=recv_sem,
            device_id=peer, device_id_type=MESH).start()

    def done(ref, sem):
        pltpu.make_async_copy(ref, ref, sem).wait()

    def taken(pieces, sem):
        some = {1: zbuf.at[0, 0, 0], 2: zbuf.at[0, 0], 4: zbuf.at[0], 6: zbuf.at[pl.ds(0, 3), 0],
                8: zbuf.at[pl.ds(0, 2)], 30: pbuf.at[0, pl.ds(0, 15)], 60: zbuf.at[pl.ds(0, 15)]}
        done(some[pieces], sem)

    def tiles(count, sem):
        done(part.at[pl.ds(0, count)], sem)

    def z_ref(dz, who, n):
        return zbuf.at[slot_z(dz), who, n]

    def z_shift(way, step):
        return step * (2 * way - 1)

    def z_on(way, step, who, n):
        src = z_ref(z_shift(way, step), who, n)
        send(src, src, step_send.at[who, step % 2], z_recv.at[way, step, who, n], at_z(1 - 2 * way, 1))

    def z_share(dz, who, n, send_sem):
        src = z_ref(dz, who, n)
        send(src, src, send_sem, s_recv.at[(dz + NZ) % NZ], sibling)

    def z_step(who, step, on=lambda way, n: True):
        for n in range(2):
            for way in range(2):
                taken(1, z_recv.at[way, step - 1, who, n])
                if on(way, n):
                    z_on(way, step, who, n)
                z_share(z_shift(way, step), who, n, step_send.at[who, step % 2])

    def z_last(who):
        for n in range(2):
            taken(1, z_recv.at[n, FAR - 1, who, n])
            z_share(FAR, who, n, last_send)

    def last_hop(way, n):
        return way == n

    def p_xy(who, n, a, b):
        f = (1 - 2 * who) * (1 - 2 * n)
        return f * ((1 - n) * a + n * b), f * ((1 - n) * b + n * a)

    def p_ref(who, n, a, b):
        return pbuf.at[who, slot_xy(*p_xy(who, n, a, b)), n]

    def p_at(a):
        return (a + 4) % 4

    def p_first(src, who, n, a, way):
        send(src, p_ref(who, n, a, 0), p_send, p_recv.at[who, p_at(a - way), 0],
             at_xy(*p_xy(who, n, way, 0), 0))

    def p_second(src, who, n, a, b, way):
        send(src, p_ref(who, n, a, b), p_send, p_recv.at[who, p_at(a), p_at(b - way)],
             at_xy(*p_xy(who, n, 0, way), 0))

    def p_share(who, a, b):
        @pl.when(who == 1)
        def _():
            for n in range(2):
                src = p_ref(who, n, a, b)
                send(src, src, q_send, q_recv, sibling)

    def each(body):
        def step(who, carry):
            body(who)
            return carry
        lax.fori_loop(0, 2, step, 0)

    @pl.when(core == 1)
    def _():
        for n in range(2):
            z_on(0, 0, 1, n)
            z_on(1, 0, 1, n)

    for n in range(2):
        z_share(0, core, n, share_send)
    own_copies = [
        pltpu.make_async_copy(zbuf.at[z, core, n], pbuf.at[core, row, n], own_sem.at[n]) for n in range(2)]
    for copy in own_copies:
        copy.start()

    def own_part():
        squares = jnp.zeros((8, BLK), F32)
        diag = jnp.zeros((8, BLK), F32)
        eye = (lax.broadcasted_iota(jnp.int32, (BLK, BLK), 0)
               == lax.broadcasted_iota(jnp.int32, (BLK, BLK), 1)).astype(F32)
        for i in range(ROWS):
            n, k = i // 2, i % 2
            blk = zbuf[z, core, n, k * BLK:(k + 1) * BLK, :].astype(F32)
            squares += jnp.sum((blk * blk).reshape(BLK // 8, 8, BLK), axis=0)
            on_diag = (col == row * 2 + n).astype(F32)
            diag += jnp.sum((blk * eye).reshape(BLK // 8, 8, BLK), axis=0) * on_diag
            twice = blk * (2.0 - 2.0 * odd)
            out_ref[i, 0] = twice * (1.0 - spots[i])
            out_ref[i, 1] = twice * spots[i]
        tot[0] = sign * squares + (2.0 - 2.0 * odd) * diag

    def t_copy(k, src, sem, peer):
        send(tot.at[src], part.at[k], t_send, t_recv.at[sem], peer)

    def t_add(src, dst, ks, sem):
        total = tot[src]
        tiles(len(ks), t_recv.at[sem])
        for k in ks:
            total += part[k]
        tot[dst] = total

    def spread(i):
        return ((i + 1) // 2) * (1 - 2 * (i % 2))

    def compute(i, count):
        for g in range(count):
            slot = slot_z(spread(i + g))
            for n in range(2):
                for who in range(2):
                    marks = zbuf[slot, who, n, PAIR:, :].astype(F32)
                    for k in range(2):
                        spot = jnp.broadcast_to(marks[k:k + 1], (16, BLK)) * sign
                        blk = zbuf[slot, who, n, k * BLK:(k + 1) * BLK, :].reshape(BLK // 16, 16, BLK)
                        r, c = (2 * n + k) * BLK, (2 * g + who) * PAIR
                        lhs[r:r + BLK, c:c + BLK] = (blk * (sign - spot).astype(BF16)[None]).reshape(BLK, BLK)
                        lhs[r:r + BLK, c + BLK:c + PAIR] = (blk * spot.astype(BF16)[None]).reshape(BLK, BLK)
                marks = pbuf[core, slot, n, PAIR:, :].astype(F32)
                for k in range(2):
                    spot = jnp.broadcast_to(marks[k:k + 1], (16, BLK))
                    blk = pbuf[core, slot, n, k * BLK:(k + 1) * BLK, :].reshape(BLK // 16, 16, BLK)
                    r = (ROWS * g + 2 * n + k) * BLK
                    rhs[r:r + BLK, :BLK] = (blk * (1.0 - spot).astype(BF16)[None]).reshape(BLK, BLK)
                    rhs[r:r + BLK, BLK:] = (blk * spot.astype(BF16)[None]).reshape(BLK, BLK)
        depth = count * ROWS * BLK
        prod = jnp.dot(lhs[:, :depth], rhs[:depth, :], preferred_element_type=F32)
        for r in range(ROWS):
            for j in range(2):
                out_ref[r, j] += prod[r * BLK:(r + 1) * BLK, j * BLK:(j + 1) * BLK]

    def loop(lo, hi, body):
        def step(i, carry):
            body(i)
            return carry
        lax.fori_loop(lo, hi, step, 0)

    @pl.when(core == 1)
    def _():
        own_part()
        t_copy(0, 0, 0, sibling)
        z_step(1, 1)
        taken(2, s_recv.at[0])
        for n in range(2):
            z_on(0, 0, 0, n)
            z_on(1, 0, 0, n)
        taken(4, step_send.at[1, 0])

        def ring(step):
            z_step(1, step)
            z_step(0, step - 1)

            @pl.when(step == 5)
            def _():
                tiles(1, t_recv.at[3])
                tot[1] = part[7]
                for k in range(3):
                    t_copy(8 + k, 1, 4, at_z(1 + k, 1))

            @pl.when(step == 6)
            def _():
                t_add(1, 2, (8, 9, 10), 4)
                t_copy(11, 2, 5, at_z(4, 1))
                t_copy(12, 2, 6, at_z(-4, 1))

            taken(8, step_send.at[1, (step - 1) % 2])

            @pl.when(step == 2)
            def _():
                taken(4, step_send.at[0, 0])

            @pl.when(step > 2)
            def _():
                taken(8, step_send.at[0, step % 2])

        loop(2, 7, ring)
        taken(2, share_send)
        taken(30, q_recv)
        for copy in own_copies:
            copy.wait()

    @pl.when(core == 0)
    def _():
        def p_begin(who, n):
            src = zbuf.at[z, who, n]
            for way in (1, -1):
                p_first(src, who, n, 0, way)
                p_second(src, who, n, 0, 0, way)

        def take(who, a, b):
            taken(2, p_recv.at[who, p_at(a), p_at(b)])
            p_share(who, a, b)

        def first(a):
            def body(who):
                taken(2, p_recv.at[who, p_at(a), 0])
                for n in range(2):
                    src = p_ref(who, n, a, 0)
                    if a == -1:
                        p_first(src, who, n, a, 1)
                    p_second(src, who, n, a, 0, 1)
                    p_second(src, who, n, a, 0, -1)
                p_share(who, a, 0)
            each(body)

        def second(a):
            def body(who):
                taken(2, p_recv.at[who, p_at(a), p_at(-1)])
                for n in range(2):
                    p_second(p_ref(who, n, a, -1), who, n, a, -1, 1)
                p_share(who, a, -1)
            each(body)

        for n in range(2):
            p_begin(0, n)
        own_part()
        taken(2, s_recv.at[0])
        for n in range(2):
            p_begin(1, n)
        t_add(0, 1, (0,), 0)
        for k in range(3):
            t_copy(1 + k, 1, 1, at_xy(1 + k, 0, 0))
        t_add(1, 2, (1, 2, 3), 1)
        for k in range(3):
            t_copy(4 + k, 2, 2, at_xy(0, 1 + k, 0))
        first(-1)
        first(1)
        t_add(2, 3, (4, 5, 6), 2)
        t_copy(7, 3, 3, sibling)
        first(2)
        second(0)
        second(-1)
        second(1)
        second(2)
        for b in (1, 2):
            for a in (0, -1, 1, 2):
                each(lambda who, a=a, b=b: take(who, a, b))
        for copy in own_copies:
            copy.wait()
        taken(2, share_send)
        taken(60, p_send)
        taken(30, q_send)
        tiles(7, t_send)

    def z_taken(i, count):
        @pl.when(core == 0)
        def _():
            for g in range(count):
                taken(4, s_recv.at[(spread(i + g) + NZ) % NZ])

    def four(i):
        @pl.when((core == 1) & (i == 2))
        def _():
            z_step(1, 7, last_hop)
            z_step(0, 6)
            tiles(1, t_recv.at[5])
            send(part.at[11], part.at[13], t_send, t_recv.at[6], at_z(4, 1))
            taken(8, step_send.at[1, 0])
            taken(8, step_send.at[0, 1])

        @pl.when(i == 0)
        def _():
            z_taken(1, 3)

        @pl.when(i > 0)
        def _():
            z_taken(4 * i, 4)

        compute(4 * i, 4)

    loop(0, 3, four)

    @pl.when(core == 1)
    def _():
        z_last(1)
        z_step(0, 7, last_hop)

    z_taken(12, 2)
    compute(12, 2)

    def one(i):
        @pl.when((core == 1) & (i == 14))
        def _():
            z_last(0)

        z_taken(i, 1)
        compute(i, 1)

    loop(14, 16, one)

    @pl.when(core == 1)
    def _():
        tail = tot[2] + part[11]
        tiles(2, t_recv.at[6])
        for k in (12, 13):
            tail += part[k]
        tot[3] = tail
        t_copy(14, 3, 7, sibling)
        tot[4] = tail
        taken(6, step_send.at[1, 1])
        taken(8, step_send.at[0, 0])
        taken(6, step_send.at[0, 1])
        taken(4, last_send)
        tiles(8, t_send)

    @pl.when(core == 0)
    def _():
        tiles(1, t_recv.at[7])
        tot[4] = part[14]

    total = jnp.sum(jnp.sum(tot[4], axis=0, keepdims=True), axis=1, keepdims=True)
    occ_ref[...] = jnp.broadcast_to(total / (NX * NY * ROWS * BLK), occ_ref.shape)


def on_device(pattern, values, branch_sign):
    purified, occupation = pl.pallas_call(
        kernel,
        out_shape=(
            jax.ShapeDtypeStruct((ROWS, 2, BLK, BLK), F32),
            jax.ShapeDtypeStruct((8, BLK), F32),
        ),
        in_specs=[
            pl.BlockSpec(memory_space=pltpu.HBM),
            pl.BlockSpec(memory_space=pltpu.SMEM),
            pl.BlockSpec(memory_space=pltpu.HBM),
        ],
        out_specs=(
            pl.BlockSpec(memory_space=pltpu.VMEM),
            pl.BlockSpec(memory_space=pltpu.VMEM),
        ),
        scratch_shapes=[
            pltpu.VMEM((NZ, 2, 2, HALF, BLK), BF16),
            pltpu.VMEM((2, NX * NY, 2, HALF, BLK), BF16),
            pltpu.VMEM((ROWS * BLK, 4 * ROWS * BLK), BF16),
            pltpu.VMEM((4 * ROWS * BLK, PAIR), BF16),
            pltpu.VMEM((5, 8, BLK), F32),
            pltpu.VMEM((15, 8, BLK), F32),
            pltpu.SMEM((1, ROWS), jnp.int32),
            pltpu.SemaphoreType.DMA((2,)),
            pltpu.SemaphoreType.DMA((1,)),
            pltpu.SemaphoreType.DMA((2,)),
            pltpu.SemaphoreType.DMA((2, 2)),
            pltpu.SemaphoreType.DMA,
            pltpu.SemaphoreType.DMA,
            pltpu.SemaphoreType.DMA((2, FAR, 2, 2)),
            pltpu.SemaphoreType.DMA((NZ,)),
            pltpu.SemaphoreType.DMA,
            pltpu.SemaphoreType.DMA((2, 4, 4)),
            pltpu.SemaphoreType.DMA,
            pltpu.SemaphoreType.DMA,
            pltpu.SemaphoreType.DMA,
            pltpu.SemaphoreType.DMA((8,)),
        ],
        compiler_params=pltpu.CompilerParams(
            collective_id=0, has_side_effects=True, vmem_limit_bytes=32 * 1024 * 1024),
        cost_estimate=pl.CostEstimate(flops=2 * 512 * 8192 * 256, bytes_accessed=1 << 20, transcendentals=0),
    )(pltpu.with_memory_space_constraint(pattern.reshape(1, ROWS), pltpu.HBM), branch_sign,
      pltpu.with_memory_space_constraint(values.reshape(ROWS * BLK, BLK), pltpu.HBM))
    return purified, occupation[0, 0]


def solution(mesh):
    in_specs = (P("row", "col"), P("row", "col", None, None), P())
    out_specs = (P("row", "col", None, None), P())
    return jax.shard_map(
        on_device, mesh=mesh, in_specs=in_specs, out_specs=out_specs, check_vma=False)
```

```python
import jax
import jax.numpy as jnp
from jax import lax
from jax.experimental import pallas as pl
from jax.experimental.pallas import tpu as pltpu
from jax.sharding import PartitionSpec as P

MESH = pl.DeviceIdType.MESH
NX, NY, NZ = 4, 4, 16
BLK = 128
ROWS = 4
PAIR = 2 * BLK
HALF = PAIR + 16
FAR = NZ // 2
F32 = jnp.float32
BF16 = jnp.bfloat16


def kernel(pat_hbm, sign_ref, val_ref, out_ref, occ_ref,
           zbuf, pbuf, lhs, rhs, tot, part, pat_ref, load_sem, small_sem, own_sem,
           step_send, last_send, share_send, z_recv, s_recv, p_send, p_recv, q_send, q_recv, t_send, t_recv):
    row = lax.axis_index("row")
    col = lax.axis_index("col")
    y, x = lax.div(row, NX), lax.rem(row, NX)
    z, core = lax.div(col, 2), lax.rem(col, 2)

    def slot_z(dz):
        return lax.rem(z + dz + NZ, NZ)

    def slot_xy(dx, dy):
        return lax.rem(y + dy + NY, NY) * NX + lax.rem(x + dx + NX, NX)

    def at_z(dz, who):
        return (row, slot_z(dz) * 2 + who)

    def at_xy(dx, dy, who):
        return (slot_xy(dx, dy), z * 2 + who)

    sibling = (row, z * 2 + 1 - core)

    barrier = pltpu.get_barrier_semaphore()

    def greet(peers):
        for peer in peers:
            pl.semaphore_signal(barrier, inc=1, device_id=peer, device_id_type=MESH)

    @pl.when(core == 1)
    def _():
        greet([at_z(-1, 1), at_z(1, 1)])

    greet([sibling])

    @pl.when(core == 0)
    def _():
        greet([at_xy(1, 0, 0), at_xy(-1, 0, 0), at_xy(0, 1, 0), at_xy(0, -1, 0), at_xy(2, 0, 0), at_xy(0, 2, 0)])

    small = pltpu.make_async_copy(pat_hbm, pat_ref, small_sem.at[0])
    small.start()
    loads = [
        pltpu.make_async_copy(
            val_ref.at[pl.ds(n * PAIR, PAIR)], zbuf.at[z, core, n, pl.ds(0, PAIR)], load_sem.at[n])
        for n in range(2)
    ]
    for load in loads:
        load.start()

    small.wait()
    odd = (sign_ref[0] % 2).astype(F32)
    sign = 2.0 * odd - 1.0
    spots = [pat_ref[0, i].astype(F32) for i in range(ROWS)]
    tile_row = lax.broadcasted_iota(jnp.int32, (16, BLK), 0)
    for n in range(2):
        marks = jnp.where(tile_row == 0, spots[2 * n], jnp.where(tile_row == 1, spots[2 * n + 1], 0.0))
        zbuf[z, core, n, PAIR:, :] = marks.astype(BF16)
    for load in loads:
        load.wait()

    @pl.when(core == 0)
    def _():
        pl.semaphore_wait(barrier, 7)

    @pl.when(core == 1)
    def _():
        pl.semaphore_wait(barrier, 3)

    def send(src, dst, send_sem, recv_sem, peer):
        pltpu.make_async_remote_copy(
            src_ref=src, dst_ref=dst, send_sem=send_sem, recv_sem=recv_sem,
            device_id=peer, device_id_type=MESH).start()

    def done(ref, sem):
        pltpu.make_async_copy(ref, ref, sem).wait()

    def taken(pieces, sem):
        some = {1: zbuf.at[0, 0, 0], 2: zbuf.at[0, 0], 4: zbuf.at[0], 6: zbuf.at[pl.ds(0, 3), 0],
                8: zbuf.at[pl.ds(0, 2)], 30: pbuf.at[0, pl.ds(0, 15)], 60: zbuf.at[pl.ds(0, 15)]}
        done(some[pieces], sem)

    def tiles(count, sem):
        done(part.at[pl.ds(0, count)], sem)

    def z_ref(dz, who, n):
        return zbuf.at[slot_z(dz), who, n]

    def z_shift(way, step):
        return step * (2 * way - 1)

    def z_on(way, step, who, n):
        src = z_ref(z_shift(way, step), who, n)
        send(src, src, step_send.at[who, step % 2], z_recv.at[way, step, who, n], at_z(1 - 2 * way, 1))

    def z_share(dz, who, n, send_sem):
        src = z_ref(dz, who, n)
        send(src, src, send_sem, s_recv.at[(dz + NZ) % NZ], sibling)

    def z_step(who, step, on=lambda way, n: True):
        for n in range(2):
            for way in range(2):
                taken(1, z_recv.at[way, step - 1, who, n])
                if on(way, n):
                    z_on(way, step, who, n)
                z_share(z_shift(way, step), who, n, step_send.at[who, step % 2])

    def z_last(who):
        for n in range(2):
            taken(1, z_recv.at[n, FAR - 1, who, n])
            z_share(FAR, who, n, last_send)

    def last_hop(way, n):
        return way == n

    def p_xy(who, n, a, b):
        f = (1 - 2 * who) * (1 - 2 * n)
        return f * ((1 - n) * a + n * b), f * ((1 - n) * b + n * a)

    def p_ref(who, n, a, b):
        return pbuf.at[who, slot_xy(*p_xy(who, n, a, b)), n]

    def p_at(a):
        return (a + 4) % 4

    def p_first(src, who, n, a, way):
        send(src, p_ref(who, n, a, 0), p_send, p_recv.at[who, p_at(a - way), 0],
             at_xy(*p_xy(who, n, way, 0), 0))

    def p_second(src, who, n, a, b, way):
        send(src, p_ref(who, n, a, b), p_send, p_recv.at[who, p_at(a), p_at(b - way)],
             at_xy(*p_xy(who, n, 0, way), 0))

    def p_share(who, a, b):
        if who == 1:
            for n in range(2):
                src = p_ref(who, n, a, b)
                send(src, src, q_send, q_recv, sibling)

    def each(body):
        for who in range(2):
            body(who)

    @pl.when(core == 1)
    def _():
        for n in range(2):
            z_on(0, 0, 1, n)
            z_on(1, 0, 1, n)

    for n in range(2):
        z_share(0, core, n, share_send)
    own_copies = [
        pltpu.make_async_copy(zbuf.at[z, core, n], pbuf.at[core, row, n], own_sem.at[n]) for n in range(2)]
    for copy in own_copies:
        copy.start()

    def own_part():
        squares = jnp.zeros((8, BLK), F32)
        diag = jnp.zeros((8, BLK), F32)
        eye = (lax.broadcasted_iota(jnp.int32, (BLK, BLK), 0)
               == lax.broadcasted_iota(jnp.int32, (BLK, BLK), 1)).astype(F32)
        for i in range(ROWS):
            n, k = i // 2, i % 2
            blk = zbuf[z, core, n, k * BLK:(k + 1) * BLK, :].astype(F32)
            squares += jnp.sum((blk * blk).reshape(BLK // 8, 8, BLK), axis=0)
            on_diag = (col == row * 2 + n).astype(F32)
            diag += jnp.sum((blk * eye).reshape(BLK // 8, 8, BLK), axis=0) * on_diag
            twice = blk * (2.0 - 2.0 * odd)
            out_ref[i, 0] = twice * (1.0 - spots[i])
            out_ref[i, 1] = twice * spots[i]
        tot[0] = sign * squares + (2.0 - 2.0 * odd) * diag

    def t_copy(k, src, sem, peer):
        send(tot.at[src], part.at[k], t_send, t_recv.at[sem], peer)

    def t_add(src, dst, ks, sem):
        total = tot[src]
        tiles(len(ks), t_recv.at[sem])
        for k in ks:
            total += part[k]
        tot[dst] = total

    def spread(i):
        return ((i + 1) // 2) * (1 - 2 * (i % 2))

    def compute(i, count):
        for g in range(count):
            slot = slot_z(spread(i + g))
            for n in range(2):
                for who in range(2):
                    marks = zbuf[slot, who, n, PAIR:, :].astype(F32)
                    for k in range(2):
                        spot = jnp.broadcast_to(marks[k:k + 1], (16, BLK)) * sign
                        blk = zbuf[slot, who, n, k * BLK:(k + 1) * BLK, :].reshape(BLK // 16, 16, BLK)
                        r, c = (2 * n + k) * BLK, (2 * g + who) * PAIR
                        lhs[r:r + BLK, c:c + BLK] = (blk * (sign - spot).astype(BF16)[None]).reshape(BLK, BLK)
                        lhs[r:r + BLK, c + BLK:c + PAIR] = (blk * spot.astype(BF16)[None]).reshape(BLK, BLK)
                marks = pbuf[core, slot, n, PAIR:, :].astype(F32)
                for k in range(2):
                    spot = jnp.broadcast_to(marks[k:k + 1], (16, BLK))
                    blk = pbuf[core, slot, n, k * BLK:(k + 1) * BLK, :].reshape(BLK // 16, 16, BLK)
                    r = (ROWS * g + 2 * n + k) * BLK
                    rhs[r:r + BLK, :BLK] = (blk * (1.0 - spot).astype(BF16)[None]).reshape(BLK, BLK)
                    rhs[r:r + BLK, BLK:] = (blk * spot.astype(BF16)[None]).reshape(BLK, BLK)
        depth = count * ROWS * BLK
        prod = jnp.dot(lhs[:, :depth], rhs[:depth, :], preferred_element_type=F32)
        for r in range(ROWS):
            for j in range(2):
                out_ref[r, j] += prod[r * BLK:(r + 1) * BLK, j * BLK:(j + 1) * BLK]

    def loop(lo, hi, body):
        def step(i, carry):
            body(i)
            return carry
        lax.fori_loop(lo, hi, step, 0)

    @pl.when(core == 1)
    def _():
        own_part()
        t_copy(0, 0, 0, sibling)
        z_step(1, 1)
        taken(2, s_recv.at[0])
        for n in range(2):
            z_on(0, 0, 0, n)
            z_on(1, 0, 0, n)
        taken(4, step_send.at[1, 0])

        def ring(step):
            z_step(1, step)
            z_step(0, step - 1)

            @pl.when(step == 5)
            def _():
                tiles(1, t_recv.at[3])
                tot[1] = part[7]
                for k in range(3):
                    t_copy(8 + k, 1, 4, at_z(1 + k, 1))

            @pl.when(step == 6)
            def _():
                t_add(1, 2, (8, 9, 10), 4)
                t_copy(11, 2, 5, at_z(4, 1))
                t_copy(12, 2, 6, at_z(-4, 1))

            taken(8, step_send.at[1, (step - 1) % 2])

            @pl.when(step == 2)
            def _():
                taken(4, step_send.at[0, 0])

            @pl.when(step > 2)
            def _():
                taken(8, step_send.at[0, step % 2])

        loop(2, 7, ring)
        z_step(1, 7, last_hop)
        z_step(0, 6)
        tiles(1, t_recv.at[5])
        send(part.at[11], part.at[13], t_send, t_recv.at[6], at_z(4, 1))
        taken(2, share_send)
        taken(30, q_recv)
        for copy in own_copies:
            copy.wait()
        taken(8, step_send.at[1, 0])
        taken(8, step_send.at[0, 1])

    @pl.when(core == 0)
    def _():
        def p_begin(who, n):
            src = zbuf.at[z, who, n]
            for way in (1, -1):
                p_first(src, who, n, 0, way)
                p_second(src, who, n, 0, 0, way)

        def take(who, a, b):
            taken(2, p_recv.at[who, p_at(a), p_at(b)])
            p_share(who, a, b)

        def first(a):
            def body(who):
                taken(2, p_recv.at[who, p_at(a), 0])
                for n in range(2):
                    src = p_ref(who, n, a, 0)
                    if a == -1:
                        p_first(src, who, n, a, 1)
                    p_second(src, who, n, a, 0, 1)
                    p_second(src, who, n, a, 0, -1)
                p_share(who, a, 0)
            each(body)

        def second(a):
            def body(who):
                taken(2, p_recv.at[who, p_at(a), p_at(-1)])
                for n in range(2):
                    p_second(p_ref(who, n, a, -1), who, n, a, -1, 1)
                p_share(who, a, -1)
            each(body)

        for n in range(2):
            p_begin(0, n)
        own_part()
        taken(2, s_recv.at[0])
        for n in range(2):
            p_begin(1, n)
        t_add(0, 1, (0,), 0)
        for k in range(3):
            t_copy(1 + k, 1, 1, at_xy(1 + k, 0, 0))
        first(-1)
        first(1)
        t_add(1, 2, (1, 2, 3), 1)
        for k in range(3):
            t_copy(4 + k, 2, 2, at_xy(0, 1 + k, 0))
        first(2)
        second(0)
        t_add(2, 3, (4, 5, 6), 2)
        t_copy(7, 3, 3, sibling)
        second(-1)
        second(1)
        second(2)
        for b in (1, 2):
            for a in (0, -1, 1, 2):
                each(lambda who, a=a, b=b: take(who, a, b))
        for copy in own_copies:
            copy.wait()
        taken(2, share_send)
        taken(60, p_send)
        taken(30, q_send)
        tiles(7, t_send)

    def z_taken(i, count):
        @pl.when(core == 0)
        def _():
            for g in range(count):
                taken(4, s_recv.at[(spread(i + g) + NZ) % NZ])

    def four(i):
        @pl.when((core == 1) & (i == 2))
        def _():
            z_last(1)
            z_step(0, 7, last_hop)

        @pl.when(i == 0)
        def _():
            z_taken(1, 3)

        @pl.when(i > 0)
        def _():
            z_taken(4 * i, 4)

        compute(4 * i, 4)

    loop(0, 3, four)

    z_taken(12, 2)
    compute(12, 2)

    def one(i):
        @pl.when((core == 1) & (i == 15))
        def _():
            z_last(0)
            tail = tot[2] + part[11]
            tiles(2, t_recv.at[6])
            for k in (12, 13):
                tail += part[k]
            tot[3] = tail
            t_copy(14, 3, 7, sibling)
            tot[4] = tail

        z_taken(i, 1)
        compute(i, 1)

    loop(14, 16, one)

    @pl.when(core == 1)
    def _():
        taken(6, step_send.at[1, 1])
        taken(8, step_send.at[0, 0])
        taken(6, step_send.at[0, 1])
        taken(4, last_send)
        tiles(8, t_send)

    @pl.when(core == 0)
    def _():
        tiles(1, t_recv.at[7])
        tot[4] = part[14]

    total = jnp.sum(jnp.sum(tot[4], axis=0, keepdims=True), axis=1, keepdims=True)
    occ_ref[...] = jnp.broadcast_to(total / (NX * NY * ROWS * BLK), occ_ref.shape)


def on_device(pattern, values, branch_sign):
    purified, occupation = pl.pallas_call(
        kernel,
        out_shape=(
            jax.ShapeDtypeStruct((ROWS, 2, BLK, BLK), F32),
            jax.ShapeDtypeStruct((8, BLK), F32),
        ),
        in_specs=[
            pl.BlockSpec(memory_space=pltpu.HBM),
            pl.BlockSpec(memory_space=pltpu.SMEM),
            pl.BlockSpec(memory_space=pltpu.HBM),
        ],
        out_specs=(
            pl.BlockSpec(memory_space=pltpu.VMEM),
            pl.BlockSpec(memory_space=pltpu.VMEM),
        ),
        scratch_shapes=[
            pltpu.VMEM((NZ, 2, 2, HALF, BLK), BF16),
            pltpu.VMEM((2, NX * NY, 2, HALF, BLK), BF16),
            pltpu.VMEM((ROWS * BLK, 4 * ROWS * BLK), BF16),
            pltpu.VMEM((4 * ROWS * BLK, PAIR), BF16),
            pltpu.VMEM((5, 8, BLK), F32),
            pltpu.VMEM((15, 8, BLK), F32),
            pltpu.SMEM((1, ROWS), jnp.int32),
            pltpu.SemaphoreType.DMA((2,)),
            pltpu.SemaphoreType.DMA((1,)),
            pltpu.SemaphoreType.DMA((2,)),
            pltpu.SemaphoreType.DMA((2, 2)),
            pltpu.SemaphoreType.DMA,
            pltpu.SemaphoreType.DMA,
            pltpu.SemaphoreType.DMA((2, FAR, 2, 2)),
            pltpu.SemaphoreType.DMA((NZ,)),
            pltpu.SemaphoreType.DMA,
            pltpu.SemaphoreType.DMA((2, 4, 4)),
            pltpu.SemaphoreType.DMA,
            pltpu.SemaphoreType.DMA,
            pltpu.SemaphoreType.DMA,
            pltpu.SemaphoreType.DMA((8,)),
        ],
        compiler_params=pltpu.CompilerParams(
            collective_id=0, has_side_effects=True, vmem_limit_bytes=32 * 1024 * 1024),
        cost_estimate=pl.CostEstimate(flops=2 * 512 * 8192 * 256, bytes_accessed=1 << 20, transcendentals=0),
    )(pltpu.with_memory_space_constraint(pattern.reshape(1, ROWS), pltpu.HBM), branch_sign,
      pltpu.with_memory_space_constraint(values.reshape(ROWS * BLK, BLK), pltpu.HBM))
    return purified, occupation[0, 0]


def solution(mesh):
    in_specs = (P("row", "col"), P("row", "col", None, None), P())
    out_specs = (P("row", "col", None, None), P())
    return jax.shard_map(
        on_device, mesh=mesh, in_specs=in_specs, out_specs=out_specs, check_vma=False)
```

```python
import jax
import jax.numpy as jnp
from jax import lax
from jax.experimental import pallas as pl
from jax.experimental.pallas import tpu as pltpu
from jax.sharding import PartitionSpec as P

MESH = pl.DeviceIdType.MESH
NX, NY, NZ = 4, 4, 16
BLK = 128
ROWS = 4
PAIR = 2 * BLK
HALF = PAIR + 16
FAR = NZ // 2
F32 = jnp.float32
BF16 = jnp.bfloat16


def kernel(pat_hbm, sign_ref, val_ref, out_ref, occ_ref,
           zbuf, pbuf, lhs, rhs, tot, part, pat_ref, load_sem, small_sem, own_sem,
           step_send, last_send, share_send, z_recv, s_recv, p_send, p_recv, q_send, q_recv, t_send, t_recv):
    row = lax.axis_index("row")
    col = lax.axis_index("col")
    y, x = lax.div(row, NX), lax.rem(row, NX)
    z, core = lax.div(col, 2), lax.rem(col, 2)

    def slot_z(dz):
        return lax.rem(z + dz + NZ, NZ)

    def slot_xy(dx, dy):
        return lax.rem(y + dy + NY, NY) * NX + lax.rem(x + dx + NX, NX)

    def at_z(dz, who):
        return (row, slot_z(dz) * 2 + who)

    def at_xy(dx, dy, who):
        return (slot_xy(dx, dy), z * 2 + who)

    sibling = (row, z * 2 + 1 - core)

    barrier = pltpu.get_barrier_semaphore()

    def greet(peers):
        for peer in peers:
            pl.semaphore_signal(barrier, inc=1, device_id=peer, device_id_type=MESH)

    @pl.when(core == 1)
    def _():
        greet([at_z(-1, 1), at_z(1, 1)])

    greet([sibling])

    @pl.when(core == 0)
    def _():
        greet([at_xy(1, 0, 0), at_xy(-1, 0, 0), at_xy(0, 1, 0), at_xy(0, -1, 0), at_xy(2, 0, 0), at_xy(0, 2, 0)])

    small = pltpu.make_async_copy(pat_hbm, pat_ref, small_sem.at[0])
    small.start()
    loads = [
        pltpu.make_async_copy(
            val_ref.at[pl.ds(n * PAIR, PAIR)], zbuf.at[z, core, n, pl.ds(0, PAIR)], load_sem.at[n])
        for n in range(2)
    ]
    for load in loads:
        load.start()

    small.wait()
    odd = (sign_ref[0] % 2).astype(F32)
    sign = 2.0 * odd - 1.0
    spots = [pat_ref[0, i].astype(F32) for i in range(ROWS)]
    tile_row = lax.broadcasted_iota(jnp.int32, (16, BLK), 0)
    for n in range(2):
        marks = jnp.where(tile_row == 0, spots[2 * n], jnp.where(tile_row == 1, spots[2 * n + 1], 0.0))
        zbuf[z, core, n, PAIR:, :] = marks.astype(BF16)
    for load in loads:
        load.wait()

    @pl.when(core == 0)
    def _():
        pl.semaphore_wait(barrier, 7)

    @pl.when(core == 1)
    def _():
        pl.semaphore_wait(barrier, 3)

    def send(src, dst, send_sem, recv_sem, peer):
        pltpu.make_async_remote_copy(
            src_ref=src, dst_ref=dst, send_sem=send_sem, recv_sem=recv_sem,
            device_id=peer, device_id_type=MESH).start()

    def done(ref, sem):
        pltpu.make_async_copy(ref, ref, sem).wait()

    def taken(pieces, sem):
        some = {1: zbuf.at[0, 0, 0], 2: zbuf.at[0, 0], 4: zbuf.at[0], 6: zbuf.at[pl.ds(0, 3), 0],
                8: zbuf.at[pl.ds(0, 2)], 30: pbuf.at[0, pl.ds(0, 15)], 60: zbuf.at[pl.ds(0, 15)]}
        done(some[pieces], sem)

    def tiles(count, sem):
        done(part.at[pl.ds(0, count)], sem)

    def z_ref(dz, who, n):
        return zbuf.at[slot_z(dz), who, n]

    def z_shift(way, step):
        return step * (2 * way - 1)

    def z_on(way, step, who, n):
        src = z_ref(z_shift(way, step), who, n)
        send(src, src, step_send.at[who, step % 2], z_recv.at[way, step, who, n], at_z(1 - 2 * way, 1))

    def z_share(dz, who, n, send_sem):
        src = z_ref(dz, who, n)
        send(src, src, send_sem, s_recv.at[(dz + NZ) % NZ], sibling)

    def z_step(who, step, on=lambda way, n: True):
        for n in range(2):
            for way in range(2):
                taken(1, z_recv.at[way, step - 1, who, n])
                if on(way, n):
                    z_on(way, step, who, n)
            for way in range(2):
                z_share(z_shift(way, step), who, n, step_send.at[who, step % 2])

    def z_last(who):
        for n in range(2):
            taken(1, z_recv.at[n, FAR - 1, who, n])
            z_share(FAR, who, n, last_send)

    def last_hop(way, n):
        return way == n

    def p_xy(who, n, a, b):
        f = (1 - 2 * who) * (1 - 2 * n)
        return f * ((1 - n) * a + n * b), f * ((1 - n) * b + n * a)

    def p_ref(who, n, a, b):
        return pbuf.at[who, slot_xy(*p_xy(who, n, a, b)), n]

    def p_at(a):
        return (a + 4) % 4

    def p_first(src, who, n, a, way):
        send(src, p_ref(who, n, a, 0), p_send, p_recv.at[who, p_at(a - way), 0],
             at_xy(*p_xy(who, n, way, 0), 0))

    def p_second(src, who, n, a, b, way):
        send(src, p_ref(who, n, a, b), p_send, p_recv.at[who, p_at(a), p_at(b - way)],
             at_xy(*p_xy(who, n, 0, way), 0))

    def p_share(who, a, b):
        if who == 1:
            for n in range(2):
                src = p_ref(who, n, a, b)
                send(src, src, q_send, q_recv, sibling)

    def each(body):
        for who in range(2):
            body(who)

    @pl.when(core == 1)
    def _():
        for n in range(2):
            z_on(0, 0, 1, n)
            z_on(1, 0, 1, n)

    for n in range(2):
        z_share(0, core, n, share_send)
    own_copies = [
        pltpu.make_async_copy(zbuf.at[z, core, n], pbuf.at[core, row, n], own_sem.at[n]) for n in range(2)]
    for copy in own_copies:
        copy.start()

    def own_part():
        squares = jnp.zeros((8, BLK), F32)
        diag = jnp.zeros((8, BLK), F32)
        eye = (lax.broadcasted_iota(jnp.int32, (BLK, BLK), 0)
               == lax.broadcasted_iota(jnp.int32, (BLK, BLK), 1)).astype(F32)
        for i in range(ROWS):
            n, k = i // 2, i % 2
            blk = zbuf[z, core, n, k * BLK:(k + 1) * BLK, :].astype(F32)
            squares += jnp.sum((blk * blk).reshape(BLK // 8, 8, BLK), axis=0)
            on_diag = (col == row * 2 + n).astype(F32)
            diag += jnp.sum((blk * eye).reshape(BLK // 8, 8, BLK), axis=0) * on_diag
            twice = blk * (2.0 - 2.0 * odd)
            out_ref[i, 0] = twice * (1.0 - spots[i])
            out_ref[i, 1] = twice * spots[i]
        tot[0] = sign * squares + (2.0 - 2.0 * odd) * diag

    def t_copy(k, src, sem, peer):
        send(tot.at[src], part.at[k], t_send, t_recv.at[sem], peer)

    def t_add(src, dst, ks, sem):
        total = tot[src]
        tiles(len(ks), t_recv.at[sem])
        for k in ks:
            total += part[k]
        tot[dst] = total

    def spread(i):
        return ((i + 1) // 2) * (1 - 2 * (i % 2))

    def compute(i, count):
        for g in range(count):
            slot = slot_z(spread(i + g))
            for n in range(2):
                for who in range(2):
                    marks = zbuf[slot, who, n, PAIR:, :].astype(F32)
                    for k in range(2):
                        spot = jnp.broadcast_to(marks[k:k + 1], (16, BLK)) * sign
                        blk = zbuf[slot, who, n, k * BLK:(k + 1) * BLK, :].reshape(BLK // 16, 16, BLK)
                        r, c = (2 * n + k) * BLK, (2 * g + who) * PAIR
                        lhs[r:r + BLK, c:c + BLK] = (blk * (sign - spot).astype(BF16)[None]).reshape(BLK, BLK)
                        lhs[r:r + BLK, c + BLK:c + PAIR] = (blk * spot.astype(BF16)[None]).reshape(BLK, BLK)
                marks = pbuf[core, slot, n, PAIR:, :].astype(F32)
                for k in range(2):
                    spot = jnp.broadcast_to(marks[k:k + 1], (16, BLK))
                    blk = pbuf[core, slot, n, k * BLK:(k + 1) * BLK, :].reshape(BLK // 16, 16, BLK)
                    r = (ROWS * g + 2 * n + k) * BLK
                    rhs[r:r + BLK, :BLK] = (blk * (1.0 - spot).astype(BF16)[None]).reshape(BLK, BLK)
                    rhs[r:r + BLK, BLK:] = (blk * spot.astype(BF16)[None]).reshape(BLK, BLK)
        depth = count * ROWS * BLK
        prod = jnp.dot(lhs[:, :depth], rhs[:depth, :], preferred_element_type=F32)
        for r in range(ROWS):
            for j in range(2):
                out_ref[r, j] += prod[r * BLK:(r + 1) * BLK, j * BLK:(j + 1) * BLK]

    def loop(lo, hi, body):
        def step(i, carry):
            body(i)
            return carry
        lax.fori_loop(lo, hi, step, 0)

    @pl.when(core == 1)
    def _():
        own_part()
        t_copy(0, 0, 0, sibling)
        z_step(1, 1)
        taken(2, s_recv.at[0])
        for n in range(2):
            z_on(0, 0, 0, n)
            z_on(1, 0, 0, n)
        taken(4, step_send.at[1, 0])

        def ring(step):
            z_step(1, step)
            z_step(0, step - 1)

            @pl.when(step == 4)
            def _():
                tiles(1, t_recv.at[3])
                tot[1] = part[7]
                for k in range(3):
                    t_copy(8 + k, 1, 4, at_z(1 + k, 1))

            @pl.when(step == 5)
            def _():
                t_add(1, 2, (8, 9, 10), 4)
                t_copy(11, 2, 5, at_z(4, 1))
                t_copy(12, 2, 6, at_z(-4, 1))

            taken(8, step_send.at[1, (step - 1) % 2])

            @pl.when(step == 2)
            def _():
                taken(4, step_send.at[0, 0])

            @pl.when(step > 2)
            def _():
                taken(8, step_send.at[0, step % 2])

        loop(2, 7, ring)
        z_step(1, 7, last_hop)
        tiles(1, t_recv.at[5])
        send(part.at[11], part.at[13], t_send, t_recv.at[6], at_z(4, 1))
        z_step(0, 6)
        taken(2, share_send)
        taken(30, q_recv)
        for copy in own_copies:
            copy.wait()
        taken(8, step_send.at[1, 0])
        taken(8, step_send.at[0, 1])

    @pl.when(core == 0)
    def _():
        def p_begin(who, n):
            src = zbuf.at[z, who, n]
            for way in (1, -1):
                p_first(src, who, n, 0, way)
                p_second(src, who, n, 0, 0, way)

        def take(who, a, b):
            taken(2, p_recv.at[who, p_at(a), p_at(b)])
            p_share(who, a, b)

        def first(a):
            def body(who):
                taken(2, p_recv.at[who, p_at(a), 0])
                for n in range(2):
                    src = p_ref(who, n, a, 0)
                    if a == -1:
                        p_first(src, who, n, a, 1)
                    p_second(src, who, n, a, 0, 1)
                    p_second(src, who, n, a, 0, -1)
                p_share(who, a, 0)
            each(body)

        def second(a):
            def body(who):
                taken(2, p_recv.at[who, p_at(a), p_at(-1)])
                for n in range(2):
                    p_second(p_ref(who, n, a, -1), who, n, a, -1, 1)
                p_share(who, a, -1)
            each(body)

        for n in range(2):
            p_begin(0, n)
        own_part()
        taken(2, s_recv.at[0])
        for n in range(2):
            p_begin(1, n)
        t_add(0, 1, (0,), 0)
        for k in range(3):
            t_copy(1 + k, 1, 1, at_xy(1 + k, 0, 0))
        first(-1)
        first(1)
        t_add(1, 2, (1, 2, 3), 1)
        for k in range(3):
            t_copy(4 + k, 2, 2, at_xy(0, 1 + k, 0))
        first(2)
        second(0)
        t_add(2, 3, (4, 5, 6), 2)
        t_copy(7, 3, 3, sibling)
        second(-1)
        second(1)
        second(2)
        for b in (1, 2):
            for a in (0, -1, 1, 2):
                each(lambda who, a=a, b=b: take(who, a, b))
        for copy in own_copies:
            copy.wait()
        taken(2, share_send)
        taken(60, p_send)
        taken(30, q_send)
        tiles(7, t_send)

    def z_taken(i, count):
        @pl.when(core == 0)
        def _():
            for g in range(count):
                taken(4, s_recv.at[(spread(i + g) + NZ) % NZ])

    def four(i):
        @pl.when((core == 1) & (i == 2))
        def _():
            z_last(1)
            z_step(0, 7, last_hop)

        @pl.when(i == 0)
        def _():
            z_taken(1, 3)

        @pl.when(i > 0)
        def _():
            z_taken(4 * i, 4)

        compute(4 * i, 4)

    loop(0, 3, four)

    z_taken(12, 3)
    compute(12, 3)

    @pl.when(core == 1)
    def _():
        z_last(0)
        tail = tot[2] + part[11]
        tiles(2, t_recv.at[6])
        for k in (12, 13):
            tail += part[k]
        tot[3] = tail
        t_copy(14, 3, 7, sibling)
        tot[4] = tail

    z_taken(15, 1)
    compute(15, 1)

    @pl.when(core == 1)
    def _():
        taken(6, step_send.at[1, 1])
        taken(8, step_send.at[0, 0])
        taken(6, step_send.at[0, 1])
        taken(4, last_send)
        tiles(8, t_send)

    @pl.when(core == 0)
    def _():
        tiles(1, t_recv.at[7])
        tot[4] = part[14]

    total = jnp.sum(jnp.sum(tot[4], axis=0, keepdims=True), axis=1, keepdims=True)
    occ_ref[...] = jnp.broadcast_to(total / (NX * NY * ROWS * BLK), occ_ref.shape)


def on_device(pattern, values, branch_sign):
    purified, occupation = pl.pallas_call(
        kernel,
        out_shape=(
            jax.ShapeDtypeStruct((ROWS, 2, BLK, BLK), F32),
            jax.ShapeDtypeStruct((8, BLK), F32),
        ),
        in_specs=[
            pl.BlockSpec(memory_space=pltpu.HBM),
            pl.BlockSpec(memory_space=pltpu.SMEM),
            pl.BlockSpec(memory_space=pltpu.HBM),
        ],
        out_specs=(
            pl.BlockSpec(memory_space=pltpu.VMEM),
            pl.BlockSpec(memory_space=pltpu.VMEM),
        ),
        scratch_shapes=[
            pltpu.VMEM((NZ, 2, 2, HALF, BLK), BF16),
            pltpu.VMEM((2, NX * NY, 2, HALF, BLK), BF16),
            pltpu.VMEM((ROWS * BLK, 4 * ROWS * BLK), BF16),
            pltpu.VMEM((4 * ROWS * BLK, PAIR), BF16),
            pltpu.VMEM((5, 8, BLK), F32),
            pltpu.VMEM((15, 8, BLK), F32),
            pltpu.SMEM((1, ROWS), jnp.int32),
            pltpu.SemaphoreType.DMA((2,)),
            pltpu.SemaphoreType.DMA((1,)),
            pltpu.SemaphoreType.DMA((2,)),
            pltpu.SemaphoreType.DMA((2, 2)),
            pltpu.SemaphoreType.DMA,
            pltpu.SemaphoreType.DMA,
            pltpu.SemaphoreType.DMA((2, FAR, 2, 2)),
            pltpu.SemaphoreType.DMA((NZ,)),
            pltpu.SemaphoreType.DMA,
            pltpu.SemaphoreType.DMA((2, 4, 4)),
            pltpu.SemaphoreType.DMA,
            pltpu.SemaphoreType.DMA,
            pltpu.SemaphoreType.DMA,
            pltpu.SemaphoreType.DMA((8,)),
        ],
        compiler_params=pltpu.CompilerParams(
            collective_id=0, has_side_effects=True, vmem_limit_bytes=32 * 1024 * 1024),
        cost_estimate=pl.CostEstimate(flops=2 * 512 * 8192 * 256, bytes_accessed=1 << 20, transcendentals=0),
    )(pltpu.with_memory_space_constraint(pattern.reshape(1, ROWS), pltpu.HBM), branch_sign,
      pltpu.with_memory_space_constraint(values.reshape(ROWS * BLK, BLK), pltpu.HBM))
    return purified, occupation[0, 0]


def solution(mesh):
    in_specs = (P("row", "col"), P("row", "col", None, None), P())
    out_specs = (P("row", "col", None, None), P())
    return jax.shard_map(
        on_device, mesh=mesh, in_specs=in_specs, out_specs=out_specs, check_vma=False)
```

```python
import jax
import jax.numpy as jnp
from jax import lax
from jax.experimental import pallas as pl
from jax.experimental.pallas import tpu as pltpu
from jax.sharding import PartitionSpec as P

MESH = pl.DeviceIdType.MESH
NX, NY, NZ = 4, 4, 16
BLK = 128
ROWS = 4
PAIR = 2 * BLK
HALF = PAIR + 16
FAR = NZ // 2
F32 = jnp.float32
BF16 = jnp.bfloat16


def kernel(pat_hbm, sign_ref, val_ref, out_ref, occ_ref,
           zbuf, pbuf, lhs, rhs, tot, part, pat_ref, load_sem, small_sem, own_sem,
           step_send, last_send, share_send, z_recv, s_recv, p_send, p_recv, q_send, q_recv, t_send, t_recv):
    row = lax.axis_index("row")
    col = lax.axis_index("col")
    y, x = lax.div(row, NX), lax.rem(row, NX)
    z, core = lax.div(col, 2), lax.rem(col, 2)

    def slot_z(dz):
        return lax.rem(z + dz + NZ, NZ)

    def slot_xy(dx, dy):
        return lax.rem(y + dy + NY, NY) * NX + lax.rem(x + dx + NX, NX)

    def at_z(dz, who):
        return (row, slot_z(dz) * 2 + who)

    def at_xy(dx, dy, who):
        return (slot_xy(dx, dy), z * 2 + who)

    sibling = (row, z * 2 + 1 - core)

    barrier = pltpu.get_barrier_semaphore()

    def greet(peers):
        for peer in peers:
            pl.semaphore_signal(barrier, inc=1, device_id=peer, device_id_type=MESH)

    @pl.when(core == 1)
    def _():
        greet([at_z(-1, 1), at_z(1, 1)])

    greet([sibling])

    @pl.when(core == 0)
    def _():
        greet([at_xy(1, 0, 0), at_xy(-1, 0, 0), at_xy(0, 1, 0), at_xy(0, -1, 0), at_xy(2, 0, 0), at_xy(0, 2, 0)])

    small = pltpu.make_async_copy(pat_hbm, pat_ref, small_sem.at[0])
    small.start()
    loads = [
        pltpu.make_async_copy(
            val_ref.at[pl.ds(n * PAIR, PAIR)], zbuf.at[z, core, n, pl.ds(0, PAIR)], load_sem.at[n])
        for n in range(2)
    ]
    for load in loads:
        load.start()

    small.wait()
    odd = (sign_ref[0] % 2).astype(F32)
    sign = 2.0 * odd - 1.0
    spots = [pat_ref[0, i].astype(F32) for i in range(ROWS)]
    tile_row = lax.broadcasted_iota(jnp.int32, (16, BLK), 0)
    for n in range(2):
        marks = jnp.where(tile_row == 0, spots[2 * n], jnp.where(tile_row == 1, spots[2 * n + 1], 0.0))
        zbuf[z, core, n, PAIR:, :] = marks.astype(BF16)
    for load in loads:
        load.wait()

    @pl.when(core == 0)
    def _():
        pl.semaphore_wait(barrier, 7)

    @pl.when(core == 1)
    def _():
        pl.semaphore_wait(barrier, 3)

    def send(src, dst, send_sem, recv_sem, peer):
        pltpu.make_async_remote_copy(
            src_ref=src, dst_ref=dst, send_sem=send_sem, recv_sem=recv_sem,
            device_id=peer, device_id_type=MESH).start()

    def done(ref, sem):
        pltpu.make_async_copy(ref, ref, sem).wait()

    def taken(pieces, sem):
        some = {1: zbuf.at[0, 0, 0], 2: zbuf.at[0, 0], 4: zbuf.at[0], 6: zbuf.at[pl.ds(0, 3), 0],
                8: zbuf.at[pl.ds(0, 2)], 16: zbuf.at[pl.ds(0, 4)], 30: pbuf.at[0, pl.ds(0, 15)], 60: zbuf.at[pl.ds(0, 15)]}
        done(some[pieces], sem)

    def tiles(count, sem):
        done(part.at[pl.ds(0, count)], sem)

    def z_ref(dz, who, n):
        return zbuf.at[slot_z(dz), who, n]

    def z_shift(way, step):
        return step * (2 * way - 1)

    def z_on(way, step, who, n):
        src = z_ref(z_shift(way, step), who, n)
        send(src, src, step_send.at[who, step % 2], z_recv.at[way, step, who, n], at_z(1 - 2 * way, 1))

    def z_share(dz, who, n, send_sem):
        src = z_ref(dz, who, n)
        send(src, src, send_sem, s_recv.at[(dz + NZ) % NZ], sibling)

    def z_step(who, step, on=lambda way, n: True):
        for n in range(2):
            for way in range(2):
                taken(1, z_recv.at[way, step - 1, who, n])
                if on(way, n):
                    z_on(way, step, who, n)
                z_share(z_shift(way, step), who, n, step_send.at[who, step % 2])

    def z_last(who):
        for n in range(2):
            taken(1, z_recv.at[n, FAR - 1, who, n])
            z_share(FAR, who, n, last_send)

    def last_hop(way, n):
        return way == n

    def p_xy(who, n, a, b):
        f = (1 - 2 * who) * (1 - 2 * n)
        return f * ((1 - n) * a + n * b), f * ((1 - n) * b + n * a)

    def p_ref(who, n, a, b):
        return pbuf.at[who, slot_xy(*p_xy(who, n, a, b)), n]

    def p_at(a):
        return (a + 4) % 4

    def p_sem(who, a, b):
        a, b = p_at(a), p_at(b)
        if b == 0:
            return 7 * who + a - 1
        if b == 3:
            return 7 * who + 3 + a
        return 14 if who == 0 else 11 + 4 * b + a

    def p_first(src, who, n, a, way):
        send(src, p_ref(who, n, a, 0), p_send, p_recv.at[p_sem(who, a - way, 0)],
             at_xy(*p_xy(who, n, way, 0), 0))

    def p_second(src, who, n, a, b, way):
        send(src, p_ref(who, n, a, b), p_send, p_recv.at[p_sem(who, a, b - way)],
             at_xy(*p_xy(who, n, 0, way), 0))

    def p_share(who, a, b):
        if who == 1:
            for n in range(2):
                src = p_ref(who, n, a, b)
                send(src, src, q_send, q_recv, sibling)

    def each(body):
        for who in range(2):
            body(who)

    @pl.when(core == 1)
    def _():
        for n in range(2):
            z_on(0, 0, 1, n)
            z_on(1, 0, 1, n)

    for n in range(2):
        z_share(0, core, n, share_send)
    own_copies = [
        pltpu.make_async_copy(zbuf.at[z, core, n], pbuf.at[core, row, n], own_sem.at[n]) for n in range(2)]
    for copy in own_copies:
        copy.start()

    def own_part():
        squares = jnp.zeros((8, BLK), F32)
        diag = jnp.zeros((8, BLK), F32)
        eye = (lax.broadcasted_iota(jnp.int32, (BLK, BLK), 0)
               == lax.broadcasted_iota(jnp.int32, (BLK, BLK), 1)).astype(F32)
        for i in range(ROWS):
            n, k = i // 2, i % 2
            blk = zbuf[z, core, n, k * BLK:(k + 1) * BLK, :].astype(F32)
            squares += jnp.sum((blk * blk).reshape(BLK // 8, 8, BLK), axis=0)
            on_diag = (col == row * 2 + n).astype(F32)
            diag += jnp.sum((blk * eye).reshape(BLK // 8, 8, BLK), axis=0) * on_diag
            twice = blk * (2.0 - 2.0 * odd)
            out_ref[i, 0] = twice * (1.0 - spots[i])
            out_ref[i, 1] = twice * spots[i]
        tot[0] = sign * squares + (2.0 - 2.0 * odd) * diag

    def t_copy(k, src, sem, peer):
        send(tot.at[src], part.at[k], t_send, t_recv.at[sem], peer)

    def t_add(src, dst, ks, sem):
        total = tot[src]
        tiles(len(ks), t_recv.at[sem])
        for k in ks:
            total += part[k]
        tot[dst] = total

    def spread(i):
        return ((i + 1) // 2) * (1 - 2 * (i % 2))

    def compute(i, count):
        for g in range(count):
            slot = slot_z(spread(i + g))
            for n in range(2):
                for who in range(2):
                    marks = zbuf[slot, who, n, PAIR:, :].astype(F32)
                    for k in range(2):
                        spot = jnp.broadcast_to(marks[k:k + 1], (16, BLK)) * sign
                        blk = zbuf[slot, who, n, k * BLK:(k + 1) * BLK, :].reshape(BLK // 16, 16, BLK)
                        r, c = (2 * n + k) * BLK, (2 * g + who) * PAIR
                        lhs[r:r + BLK, c:c + BLK] = (blk * (sign - spot).astype(BF16)[None]).reshape(BLK, BLK)
                        lhs[r:r + BLK, c + BLK:c + PAIR] = (blk * spot.astype(BF16)[None]).reshape(BLK, BLK)
                marks = pbuf[core, slot, n, PAIR:, :].astype(F32)
                for k in range(2):
                    spot = jnp.broadcast_to(marks[k:k + 1], (16, BLK))
                    blk = pbuf[core, slot, n, k * BLK:(k + 1) * BLK, :].reshape(BLK // 16, 16, BLK)
                    r = (ROWS * g + 2 * n + k) * BLK
                    rhs[r:r + BLK, :BLK] = (blk * (1.0 - spot).astype(BF16)[None]).reshape(BLK, BLK)
                    rhs[r:r + BLK, BLK:] = (blk * spot.astype(BF16)[None]).reshape(BLK, BLK)
        depth = count * ROWS * BLK
        prod = jnp.dot(lhs[:, :depth], rhs[:depth, :], preferred_element_type=F32)
        for r in range(ROWS):
            for j in range(2):
                out_ref[r, j] += prod[r * BLK:(r + 1) * BLK, j * BLK:(j + 1) * BLK]

    def loop(lo, hi, body):
        def step(i, carry):
            body(i)
            return carry
        lax.fori_loop(lo, hi, step, 0)

    @pl.when(core == 1)
    def _():
        own_part()
        t_copy(0, 0, 0, sibling)
        z_step(1, 1)
        taken(2, s_recv.at[0])
        for n in range(2):
            z_on(0, 0, 0, n)
            z_on(1, 0, 0, n)
        taken(4, step_send.at[1, 0])

        def ring(step):
            z_step(1, step)
            z_step(0, step - 1)

            @pl.when(step == 5)
            def _():
                tiles(1, t_recv.at[3])
                tot[1] = part[7]
                for k in range(3):
                    t_copy(8 + k, 1, 4, at_z(1 + k, 1))

            @pl.when(step == 6)
            def _():
                t_add(1, 2, (8, 9, 10), 4)
                t_copy(11, 2, 5, at_z(4, 1))
                t_copy(12, 2, 6, at_z(-4, 1))

            taken(8, step_send.at[1, (step - 1) % 2])

            @pl.when(step == 2)
            def _():
                taken(4, step_send.at[0, 0])

            @pl.when(step > 2)
            def _():
                taken(8, step_send.at[0, step % 2])

        loop(2, 7, ring)
        z_step(1, 7, last_hop)
        z_step(0, 6)
        tiles(1, t_recv.at[5])
        send(part.at[11], part.at[13], t_send, t_recv.at[6], at_z(4, 1))
        taken(2, share_send)
        taken(30, q_recv)
        for copy in own_copies:
            copy.wait()
        taken(8, step_send.at[1, 0])
        taken(8, step_send.at[0, 1])

    @pl.when(core == 0)
    def _():
        def p_begin(who, n):
            src = zbuf.at[z, who, n]
            for way in (1, -1):
                p_first(src, who, n, 0, way)
                p_second(src, who, n, 0, 0, way)

        def take(who, a, b):
            taken(2, p_recv.at[p_sem(who, a, b)])
            p_share(who, a, b)

        def first(a):
            def body(who):
                taken(2, p_recv.at[p_sem(who, a, 0)])
                for n in range(2):
                    src = p_ref(who, n, a, 0)
                    if a == -1:
                        p_first(src, who, n, a, 1)
                    p_second(src, who, n, a, 0, 1)
                    p_second(src, who, n, a, 0, -1)
                p_share(who, a, 0)
            each(body)

        def second(a):
            def body(who):
                taken(2, p_recv.at[p_sem(who, a, -1)])
                for n in range(2):
                    p_second(p_ref(who, n, a, -1), who, n, a, -1, 1)
                p_share(who, a, -1)
            each(body)

        for n in range(2):
            p_begin(0, n)
        own_part()
        taken(2, s_recv.at[0])
        for n in range(2):
            p_begin(1, n)
        t_add(0, 1, (0,), 0)
        for k in range(3):
            t_copy(1 + k, 1, 1, at_xy(1 + k, 0, 0))
        first(-1)
        first(1)
        t_add(1, 2, (1, 2, 3), 1)
        for k in range(3):
            t_copy(4 + k, 2, 2, at_xy(0, 1 + k, 0))
        first(2)
        second(0)
        t_add(2, 3, (4, 5, 6), 2)
        t_copy(7, 3, 3, sibling)
        second(-1)
        second(1)
        second(2)
        for b in (1, 2):
            for a in (0, -1, 1, 2):
                take(1, a, b)
        taken(16, p_recv.at[p_sem(0, 0, 1)])
        for copy in own_copies:
            copy.wait()
        taken(2, share_send)
        taken(60, p_send)
        taken(30, q_send)
        tiles(7, t_send)

    def z_taken(i, count):
        @pl.when(core == 0)
        def _():
            for g in range(count):
                taken(4, s_recv.at[(spread(i + g) + NZ) % NZ])

    def four(i):
        @pl.when((core == 1) & (i == 2))
        def _():
            z_last(1)
            z_step(0, 7, last_hop)

        @pl.when(i == 0)
        def _():
            z_taken(1, 3)

        @pl.when(i > 0)
        def _():
            z_taken(4 * i, 4)

        compute(4 * i, 4)

    loop(0, 3, four)

    z_taken(12, 2)
    compute(12, 2)

    def one(i):
        @pl.when((core == 1) & (i == 15))
        def _():
            z_last(0)
            tail = tot[2] + part[11]
            tiles(2, t_recv.at[6])
            for k in (12, 13):
                tail += part[k]
            tot[3] = tail
            t_copy(14, 3, 7, sibling)
            tot[4] = tail

        z_taken(i, 1)
        compute(i, 1)

    loop(14, 16, one)

    @pl.when(core == 1)
    def _():
        taken(6, step_send.at[1, 1])
        taken(8, step_send.at[0, 0])
        taken(6, step_send.at[0, 1])
        taken(4, last_send)
        tiles(8, t_send)

    @pl.when(core == 0)
    def _():
        tiles(1, t_recv.at[7])
        tot[4] = part[14]

    total = jnp.sum(jnp.sum(tot[4], axis=0, keepdims=True), axis=1, keepdims=True)
    occ_ref[...] = jnp.broadcast_to(total / (NX * NY * ROWS * BLK), occ_ref.shape)


def on_device(pattern, values, branch_sign):
    purified, occupation = pl.pallas_call(
        kernel,
        out_shape=(
            jax.ShapeDtypeStruct((ROWS, 2, BLK, BLK), F32),
            jax.ShapeDtypeStruct((8, BLK), F32),
        ),
        in_specs=[
            pl.BlockSpec(memory_space=pltpu.HBM),
            pl.BlockSpec(memory_space=pltpu.SMEM),
            pl.BlockSpec(memory_space=pltpu.HBM),
        ],
        out_specs=(
            pl.BlockSpec(memory_space=pltpu.VMEM),
            pl.BlockSpec(memory_space=pltpu.VMEM),
        ),
        scratch_shapes=[
            pltpu.VMEM((NZ, 2, 2, HALF, BLK), BF16),
            pltpu.VMEM((2, NX * NY, 2, HALF, BLK), BF16),
            pltpu.VMEM((ROWS * BLK, 4 * ROWS * BLK), BF16),
            pltpu.VMEM((4 * ROWS * BLK, PAIR), BF16),
            pltpu.VMEM((5, 8, BLK), F32),
            pltpu.VMEM((15, 8, BLK), F32),
            pltpu.SMEM((1, ROWS), jnp.int32),
            pltpu.SemaphoreType.DMA((2,)),
            pltpu.SemaphoreType.DMA((1,)),
            pltpu.SemaphoreType.DMA((2,)),
            pltpu.SemaphoreType.DMA((2, 2)),
            pltpu.SemaphoreType.DMA,
            pltpu.SemaphoreType.DMA,
            pltpu.SemaphoreType.DMA((2, FAR, 2, 2)),
            pltpu.SemaphoreType.DMA((NZ,)),
            pltpu.SemaphoreType.DMA,
            pltpu.SemaphoreType.DMA((23,)),
            pltpu.SemaphoreType.DMA,
            pltpu.SemaphoreType.DMA,
            pltpu.SemaphoreType.DMA,
            pltpu.SemaphoreType.DMA((8,)),
        ],
        compiler_params=pltpu.CompilerParams(
            collective_id=0, has_side_effects=True, vmem_limit_bytes=32 * 1024 * 1024),
        cost_estimate=pl.CostEstimate(flops=2 * 512 * 8192 * 256, bytes_accessed=1 << 20, transcendentals=0),
    )(pltpu.with_memory_space_constraint(pattern.reshape(1, ROWS), pltpu.HBM), branch_sign,
      pltpu.with_memory_space_constraint(values.reshape(ROWS * BLK, BLK), pltpu.HBM))
    return purified, occupation[0, 0]


def solution(mesh):
    in_specs = (P("row", "col"), P("row", "col", None, None), P())
    out_specs = (P("row", "col", None, None), P())
    return jax.shard_map(
        on_device, mesh=mesh, in_specs=in_specs, out_specs=out_specs, check_vma=False)
```
